256 devices in a mesh: pipe: 8 (over z), tensor: 32 (over x, y, core).
Axes of the slice: x: 4, y: 4, z: 8, core: 2. Of those that a mesh axis runs over, the one named last changes fastest.
Arguments:
- fresh_batch: bfloat16 [1024, 6144], P('tensor'), may hold values from -60 to 60
- handed_forward: bfloat16 [8, 1024, 6144], P('pipe', 'tensor'), may hold values from -60 to 60
- saved_inputs: bfloat16 [8, 1024, 6144], P('pipe', 'tensor'), may hold values from -60 to 60
- handed_grads: bfloat16 [8, 1024, 6144], P('pipe', 'tensor'), may hold values from -6 to 6
- loss_grad: bfloat16 [1024, 6144], P('tensor'), may hold values from -6 to 6
- norm_gain: float32 [8, 6144], P('pipe'), may hold values from 0.25 to 1.75
- route_slot: int32 [8, 2, 1024], P('pipe', None, 'tensor'), may hold values from 0 to 8, as said below
- route_weight: float32 [8, 2, 1024], P('pipe', None, 'tensor'), may hold values from 0.25 to 0.95
- w_gate: bfloat16 [8, 6144, 8192], P('pipe', None, 'tensor'), may hold values from -0.078125 to 0.078125
- w_up: bfloat16 [8, 6144, 8192], P('pipe', None, 'tensor'), may hold values from -0.078125 to 0.078125
- w_down: bfloat16 [8, 8192, 6144], P('pipe', 'tensor'), may hold values from -0.0625 to 0.0625
Outputs:
- forward_out: bfloat16 [8, 1024, 6144], P('pipe', 'tensor')
- input_grad: bfloat16 [8, 1024, 6144], P('pipe', 'tensor')
The draws below stay inside these ranges and needn't reach their ends.
Inputs may be any that keep to these rules, and one draw needn't show every extreme that they name: `route_slot`: for each layer and micro-batch, each aligned block of 32 tokens holds the slots 0 to c - 1 once each, for some c from 4 to 8, and the value 8 (token not routed to the expert) elsewhere; for each layer and micro-batch at least one block has c = 8.
All inputs are finite; a program needn't handle non-finite values.
Results may differ from the reference program's by a relative error of at most 0.007.
Values may be sent and summed in bfloat16 or wider, within the bound.
A program may use at most 128 MiB of HBM per device.

```python
import jax
import jax.numpy as jnp
from jax import lax

D = 6144
FF = 8192
TOKD = 32
LCAP = 8
TOK = 1024
CAP = 256
FFD = 256
N_PIPE = 8
N_TENSOR = 32


def spread_field(base, key, row_lo, row_hi, col_lo, col_hi):
    key_rows, key_cols = jax.random.split(key, 2)
    row_shape = base.shape[:-1] + (1,)
    rows = jnp.exp(jax.random.uniform(key_rows, row_shape, jnp.float32, jnp.log(row_lo), jnp.log(row_hi)))
    cols = jnp.exp(jax.random.uniform(key_cols, (base.shape[-1],), jnp.float32, jnp.log(col_lo), jnp.log(col_hi)))
    return (base * rows * cols).astype(jnp.bfloat16)


def activation_draw(key, shape):
    key_base, key_scale = jax.random.split(key)
    base = jnp.clip(jax.random.normal(key_base, shape, jnp.float32), -4.0, 4.0)
    return spread_field(base, key_scale, 0.3, 3.0, 0.3, 3.0)


def draw_fresh_batch(key, part):
    key = jax.random.fold_in(key, 21)
    return activation_draw(key, (TOK, D))


def draw_handed_forward(key, part):
    key = jax.random.fold_in(key, 22)
    return activation_draw(key, (N_PIPE, TOK, D))


def draw_saved_inputs(key, part):
    key = jax.random.fold_in(key, 23)
    return activation_draw(key, (N_PIPE, TOK, D))


def draw_route_slot(key, part):
    key = jax.random.fold_in(key, 11)
    key_count, key_full, key_order = jax.random.split(key, 3)
    counts = jax.random.randint(key_count, (N_PIPE, 2, N_TENSOR), LCAP // 2, LCAP + 1)
    full_block = jax.random.randint(key_full, (N_PIPE, 2), 0, N_TENSOR)
    blocks = jnp.arange(N_TENSOR, dtype=jnp.int32).reshape(1, 1, N_TENSOR)
    counts = jnp.where(blocks == full_block[:, :, None], LCAP, counts)
    keys = jax.random.split(key_order, N_PIPE * 2 * N_TENSOR)
    order = jax.vmap(lambda single: jax.random.permutation(single, TOKD))(keys)
    order = order.reshape(N_PIPE, 2, N_TENSOR, TOKD).astype(jnp.int32)
    slots = jnp.where(order < counts[..., None], order, LCAP)
    return slots.reshape(N_PIPE, 2, TOK).astype(jnp.int32)


def shard_levels(rng, extent, cuts, low, largest):
    level, own = 1.0, jax.random.fold_in(rng, 6)
    for axis_at, shards_of in cuts:
        steps = jnp.exp(jax.random.uniform(jax.random.fold_in(own, axis_at), (shards_of,), jnp.float32, low / len(cuts), largest / len(cuts)))
        level = level * jnp.repeat(steps, extent[axis_at] // shards_of).reshape([-1 if axis == axis_at else 1 for axis in range(len(extent))])
    return level


def centred(rng, extent, scale, limit, pieces=(), kind=jnp.bfloat16):
    factor_of = shard_levels(rng, extent, pieces, -0.22, 0.18) if pieces else 1.0
    entries = jax.random.normal(rng, extent, jnp.float32) * scale * factor_of
    return jnp.minimum(jnp.maximum(entries, -limit), limit).astype(kind)


def setup_inputs(seed: int = 0) -> dict:
    key_of = jax.random.split(jax.random.key(seed), 12)
    fresh_batch = draw_fresh_batch(jax.random.fold_in(key_of[11], 71), 0)
    handed_forward = draw_handed_forward(jax.random.fold_in(key_of[11], 71), 0)
    saved_inputs = draw_saved_inputs(jax.random.fold_in(key_of[11], 71), 0)
    handed_grads = centred(key_of[3], (N_PIPE, TOK, D), 1.0, 6.0, ((0, 8), (1, 32)))
    loss_grad = centred(key_of[4], (TOK, D), 1.0, 6.0, ((0, 32),))
    norm_gain = jnp.clip(1.0 + 0.15 * jax.random.normal(key_of[5], (N_PIPE, D), jnp.float32), 0.25, 1.75)
    route_slot = draw_route_slot(jax.random.fold_in(key_of[11], 71), 0)
    route_weight = jnp.clip(0.25 + 0.7 * jax.random.uniform(key_of[7], (N_PIPE, 2, TOK), jnp.float32) ** shard_levels(key_of[7], (N_PIPE, 2, TOK), ((0, 8), (2, 32)), -0.2, 0.2), 0.25, 0.95)
    w_gate = centred(key_of[8], (N_PIPE, D, FF), D ** -0.5, 0.078125, ((0, 8), (2, 32)))
    w_up = centred(key_of[9], (N_PIPE, D, FF), D ** -0.5, 0.078125, ((0, 8), (2, 32)))
    w_down = centred(key_of[10], (N_PIPE, FF, D), FF ** -0.5, 0.0625, ((0, 8), (1, 32)))
    return dict(fresh_batch=fresh_batch, handed_forward=handed_forward, saved_inputs=saved_inputs, handed_grads=handed_grads, loss_grad=loss_grad, norm_gain=norm_gain, route_slot=route_slot, route_weight=route_weight, w_gate=w_gate, w_up=w_up, w_down=w_down)


EPS = 1e-05

def normalize(field, gain):
    values = field.astype(jnp.float32)
    inverse = lax.rsqrt(lax.optimization_barrier(jnp.mean(values * values, axis=-1, keepdims=True)) + EPS)
    return (values * inverse * gain, inverse)

def selection(slots):
    places = jnp.arange(LCAP, dtype=jnp.int32).reshape(1, LCAP, 1)
    return (slots.reshape(N_TENSOR, 1, TOKD) == places).astype(jnp.float32)

def gather_rows(field, slots):
    blocks = field.reshape(N_TENSOR, TOKD, D).astype(jnp.float32)
    return jnp.einsum('jqt,jtd->jqd', selection(slots), blocks).reshape(CAP, D)

def spread_rows(rows, slots):
    blocks = rows.reshape(N_TENSOR, LCAP, D).astype(jnp.float32)
    return jnp.einsum('jqt,jqd->jtd', selection(slots), blocks).reshape(TOK, D)

def grouped_sum(pairs):
    lefts = tuple((left.reshape(CAP, N_TENSOR, FFD).transpose(1, 0, 2) for left, right in pairs))
    rights = tuple((right.reshape(N_TENSOR, FFD, D) for left, right in pairs))

    def step(total, group):
        partial_value = jnp.zeros((CAP, D), jnp.float32)
        for left, right in zip(group[0], group[1]):
            partial_value = partial_value + jnp.dot(left, right, preferred_element_type=jnp.float32)
        rounded = lax.optimization_barrier(partial_value.astype(jnp.bfloat16))
        return (total + rounded.astype(jnp.float32), None)
    total, _ = lax.scan(step, jnp.zeros((CAP, D), jnp.float32), (lefts, rights))
    return total

def reference(fresh_batch, handed_forward, saved_inputs, handed_grads, loss_grad, norm_gain, route_slot, route_weight, w_gate, w_up, w_down):
    forward_outs = []
    input_grads = []
    for section in range(N_PIPE):
        forward_in = fresh_batch if section == 0 else handed_forward[section - 1]
        grad_in = loss_grad if section == N_PIPE - 1 else handed_grads[section + 1]
        gain = norm_gain[section]
        normed_fwd = normalize(forward_in, gain)[0].astype(jnp.bfloat16)
        rows_fwd = gather_rows(normed_fwd, route_slot[section, 0]).astype(jnp.bfloat16)
        gate_fwd = jnp.dot(rows_fwd, w_gate[section], preferred_element_type=jnp.float32)
        up_fwd = jnp.dot(rows_fwd, w_up[section], preferred_element_type=jnp.float32)
        hidden = (jax.nn.silu(gate_fwd) * up_fwd).astype(jnp.bfloat16)
        expert_out = grouped_sum([(hidden, w_down[section])]).astype(jnp.bfloat16)
        spread = spread_rows(expert_out, route_slot[section, 0])
        forward_outs.append((forward_in.astype(jnp.float32) + route_weight[section, 0][:, None] * spread).astype(jnp.bfloat16))
        normed_raw, inverse = normalize(saved_inputs[section], gain)
        rows_bwd = gather_rows(normed_raw.astype(jnp.bfloat16), route_slot[section, 1]).astype(jnp.bfloat16)
        scaled_grad = (route_weight[section, 1][:, None] * grad_in.astype(jnp.float32)).astype(jnp.bfloat16)
        rows_grad = gather_rows(scaled_grad, route_slot[section, 1]).astype(jnp.bfloat16)
        gate_bwd = jnp.dot(rows_bwd, w_gate[section], preferred_element_type=jnp.float32)
        up_bwd = jnp.dot(rows_bwd, w_up[section], preferred_element_type=jnp.float32)
        grad_hidden = jnp.dot(rows_grad, w_down[section].T, preferred_element_type=jnp.float32)
        sigma = jax.nn.sigmoid(gate_bwd)
        grad_gate = (grad_hidden * up_bwd * sigma * (1.0 + gate_bwd * (1.0 - sigma))).astype(jnp.bfloat16)
        grad_up = (grad_hidden * jax.nn.silu(gate_bwd)).astype(jnp.bfloat16)
        row_grads = grouped_sum([(grad_gate, w_gate[section].T), (grad_up, w_up[section].T)]).astype(jnp.bfloat16)
        adjusted = spread_rows(row_grads, route_slot[section, 1]) * gain
        values = saved_inputs[section].astype(jnp.float32)
        result = grad_in.astype(jnp.float32) + adjusted * inverse - values * (inverse * inverse * inverse) * lax.optimization_barrier(jnp.mean(adjusted * values, axis=-1, keepdims=True))
        input_grads.append(result.astype(jnp.bfloat16))
    return (jnp.stack(forward_outs), jnp.stack(input_grads))
```

```python
import functools

import jax
import jax.numpy as jnp
from jax import lax
from jax.experimental import pallas as pl
from jax.experimental.pallas import tpu as pltpu
from jax.sharding import PartitionSpec as P

LCAP = 8
SIDE = 4
PAIR = 2 * LCAP
EPS = 1e-05
F32 = jnp.float32
BF16 = jnp.bfloat16
BWD, GRAD, FWD = 0, 1, 2
ROWG, OUT = 0, 1


def contract_last(left, right):
    return lax.dot_general(left, right, (((1,), (1,)), ((), ())), preferred_element_type=F32)


def kernel(
    n_pipe,
    fresh,
    handed_fwd,
    saved,
    handed_grads,
    loss_grad,
    gain,
    slot,
    weight,
    w_gate,
    w_up,
    w_down,
    out_fwd,
    out_grad,
    saved_v,
    fwd_v,
    grad_v,
    gain_v,
    slot_v,
    weight_v,
    wgu,
    wd,
    picked,
    tile,
    sib_tile,
    rows,
    acc,
    gh,
    act,
    part,
    sib_part,
    b_out,
    b_in,
    w_sum,
    a_out,
    a_in,
    final,
    inverse_v,
    of_v,
    og_v,
    loc_sem,
    z_send,
    z_recv,
    g_send,
    g_recv,
    r_send,
    r_recv,
):
    D = saved.shape[2]
    TOKD = saved.shape[1]
    FFD = w_down.shape[1]
    H = D // 2
    C = D // 4
    LANES = min(1024, H)

    section = lax.axis_index("pipe")
    t = lax.axis_index("tensor")
    core = t % 2
    x = t // (2 * SIDE)
    y = (t // 2) % SIDE
    a = x + core * (y - x)
    b = y + core * (x - y)
    sa = 2 * SIDE - core * (2 * SIDE - 2)
    sb = 2 + core * (2 * SIDE - 2)
    a_up, a_op, a_dn = (a + 1) % SIDE, (a + 2) % SIDE, (a + 3) % SIDE
    b_up, b_op, b_dn = (b + 1) % SIDE, (b + 2) % SIDE, (b + 3) % SIDE
    A_UP = a_up * sa + b * sb + core
    A_DN = a_dn * sa + b * sb + core
    B_UP = a * sa + b_up * sb + core
    B_DN = a * sa + b_dn * sb + core
    SIB = t + 1 - 2 * core
    Z_UP = (section + 1) % n_pipe
    Z_DN = (section + n_pipe - 1) % n_pipe
    own = pl.ds(pl.multiple_of(core * H, H), H)
    oth = pl.ds(pl.multiple_of((1 - core) * H, H), H)

    def at(tensor):
        return {"pipe": section, "tensor": tensor}

    def local(src, dst, k):
        return pltpu.make_async_copy(src, dst, loc_sem.at[k])

    first = [
        local(saved.at[0], saved_v, 0),
        local(gain, gain_v, 1),
        local(slot.at[0], slot_v, 2),
        local(weight.at[0], weight_v, 3),
    ]
    load_gu = [
        local(w_gate.at[0, own], wgu.at[0, :, pl.ds(0, FFD)], 4),
        local(w_gate.at[0, oth], wgu.at[1, :, pl.ds(0, FFD)], 5),
        local(w_up.at[0, own], wgu.at[0, :, pl.ds(FFD, FFD)], 6),
        local(w_up.at[0, oth], wgu.at[1, :, pl.ds(FFD, FFD)], 7),
    ]
    load_d = [
        local(w_down.at[0, :, own], wd.at[0], 8),
        local(w_down.at[0, :, oth], wd.at[1], 9),
    ]
    load_fresh = local(fresh, fwd_v, 10)
    load_loss = local(loss_grad, grad_v, 11)
    store_grad = local(og_v, out_grad.at[0], 12)
    store_fwd = local(of_v, out_fwd.at[0], 13)
    for copy in first:
        copy.start()

    barrier = pltpu.get_barrier_semaphore()
    for tensor in (SIB, A_UP, A_DN, B_UP, B_DN):
        pl.semaphore_signal(
            barrier, inc=1, device_id=at(tensor), device_id_type=pl.DeviceIdType.MESH
        )
    for pipe in (Z_UP, Z_DN):
        pl.semaphore_signal(
            barrier,
            inc=1,
            device_id={"pipe": pipe, "tensor": t},
            device_id_type=pl.DeviceIdType.MESH,
        )
    pl.semaphore_wait(barrier, 7)

    send_fwd = pltpu.make_async_remote_copy(
        src_ref=handed_fwd.at[0],
        dst_ref=fwd_v,
        send_sem=z_send.at[0],
        recv_sem=z_recv.at[0],
        device_id={"pipe": Z_UP, "tensor": t},
        device_id_type=pl.DeviceIdType.MESH,
    )
    send_grad = pltpu.make_async_remote_copy(
        src_ref=handed_grads.at[0],
        dst_ref=grad_v,
        send_sem=z_send.at[1],
        recv_sem=z_recv.at[1],
        device_id={"pipe": Z_DN, "tensor": t},
        device_id_type=pl.DeviceIdType.MESH,
    )

    @pl.when(section != n_pipe - 1)
    def _():
        send_fwd.start()

    @pl.when(section != 0)
    def _():
        send_grad.start()

    @pl.when(section == 0)
    def _():
        load_fresh.start()

    @pl.when(section == n_pipe - 1)
    def _():
        load_loss.start()

    sent = []

    def remote(src, dst, send_sem, recv_sem, tensor):
        copy = pltpu.make_async_remote_copy(
            src_ref=src,
            dst_ref=dst,
            send_sem=send_sem,
            recv_sem=recv_sem,
            device_id=at(tensor),
            device_id_type=pl.DeviceIdType.MESH,
        )
        return copy

    def go(copy):
        copy.start()
        sent.append(copy)
        return copy

    for copy in first:
        copy.wait()

    def row_pick(micro):
        places = lax.broadcasted_iota(jnp.int32, (PAIR, TOKD), 0) - core * LCAP
        slots = jnp.broadcast_to(slot_v[pl.ds(micro, 1), :], (PAIR, TOKD))
        return jnp.where((places == slots) & (places >= 0) & (places < LCAP), 1.0, 0.0)

    def column(row):
        wide = jnp.broadcast_to(row, (TOKD, TOKD))
        eye = lax.broadcasted_iota(jnp.int32, (TOKD, TOKD), 0) == lax.broadcasted_iota(
            jnp.int32, (TOKD, TOKD), 1
        )
        return jnp.sum(jnp.where(eye, wide, 0.0), axis=1, keepdims=True)

    def token_pick(micro):
        slots = column(slot_v[pl.ds(micro, 1), :].astype(F32))
        slots = jnp.broadcast_to(slots, (TOKD, PAIR))
        places = (
            lax.broadcasted_iota(jnp.int32, (TOKD, PAIR), 1) - core * LCAP
        ).astype(F32)
        return jnp.where(
            (places == slots) & (places >= 0.0) & (places < float(LCAP)), 1.0, 0.0
        ).astype(BF16)

    def lanes(k):
        return pl.ds(pl.multiple_of(k * LANES, LANES), LANES)

    def normed_tile(i, source, micro):
        pick = row_pick(micro).astype(BF16)

        def square(k, total):
            z = jnp.dot(pick, source[:, lanes(k)], preferred_element_type=F32)
            picked[:, lanes(k)] = z
            return total + jnp.sum(z * z, axis=1, keepdims=True)

        total = lax.fori_loop(0, D // LANES, square, jnp.zeros((PAIR, 1), F32))
        inverse = lax.rsqrt(total * (1.0 / D) + EPS)

        def scale(k, carry):
            tile[i, :, lanes(k)] = (
                picked[:, lanes(k)] * inverse * gain_v[:, lanes(k)]
            ).astype(BF16)
            return carry

        lax.fori_loop(0, D // LANES, scale, 0)

    def grad_tile(i, source, micro):
        pick_f = row_pick(micro)
        pick = pick_f.astype(BF16)
        weights = jnp.sum(
            pick_f * jnp.broadcast_to(weight_v[pl.ds(micro, 1), :], (PAIR, TOKD)),
            axis=1,
            keepdims=True,
        )

        def scale(k, carry):
            g = jnp.dot(pick, source[:, lanes(k)], preferred_element_type=F32)
            tile[i, :, lanes(k)] = (weights * g).astype(BF16)
            return carry

        lax.fori_loop(0, D // LANES, scale, 0)

    C0, C1 = pl.ds(0, C), pl.ds(C, C)

    def gather(i):
        def sems(m):
            return g_send.at[i, m], g_recv.at[i, m]

        mine = rows.at[i, 0]
        copies = {
            "tile": remote(tile.at[i, :, oth], sib_tile.at[i], *sems(0), SIB),
            "a_up": remote(mine.at[b, a], mine.at[b, a], *sems(1), A_UP),
            "a_dn": remote(mine.at[b, a], mine.at[b, a], *sems(2), A_DN),
            "a_up2": remote(
                mine.at[b, a_dn, :, C0], mine.at[b, a_dn, :, C0], *sems(3), A_UP
            ),
            "a_dn2": remote(
                mine.at[b, a_up, :, C1], mine.at[b, a_up, :, C1], *sems(4), A_DN
            ),
            "b_up": remote(mine.at[b], mine.at[b], *sems(5), B_UP),
            "b_dn": remote(mine.at[b], mine.at[b], *sems(6), B_DN),
            "b_up2": remote(
                mine.at[b_dn, :, :, C0], mine.at[b_dn, :, :, C0], *sems(7), B_UP
            ),
            "b_dn2": remote(
                mine.at[b_up, :, :, C1], mine.at[b_up, :, :, C1], *sems(8), B_DN
            ),
        }
        for m, line in enumerate((b, b_dn, b_up, b_op)):
            copies["s", m] = remote(
                mine.at[line], rows.at[i, 1, :, line], *sems(9 + m), SIB
            )
        return copies

    g = [gather(i) for i in range(3)]

    def e0(i):
        go(g[i]["tile"])

    def e1(i):
        g[i]["tile"].wait_recv()
        rows[i, 0, b, a] = tile[i, :, own] + sib_tile[i]
        go(g[i]["a_up"])
        go(g[i]["a_dn"])

    def e2(i):
        g[i]["a_up"].wait_recv()
        go(g[i]["a_up2"])
        g[i]["a_dn"].wait_recv()
        go(g[i]["a_dn2"])

    def e3(i):
        g[i]["a_up2"].wait_recv()
        g[i]["a_dn2"].wait_recv()
        go(g[i]["b_up"])
        go(g[i]["b_dn"])
        go(g[i]["s", 0])

    def e4(i):
        g[i]["b_up"].wait_recv()
        go(g[i]["b_up2"])
        go(g[i]["s", 1])
        g[i]["b_dn"].wait_recv()
        go(g[i]["b_dn2"])
        go(g[i]["s", 2])

    def e5(i):
        g[i]["b_up2"].wait_recv()
        g[i]["b_dn2"].wait_recv()
        go(g[i]["s", 3])

    def e6(i):
        for m in range(4):
            g[i]["s", m].wait_recv()

    FLAT = SIDE * SIDE * PAIR
    KC = C

    def gate_up(i):
        for h in range(2):
            for c in range(2):
                cols = pl.ds(c * KC, KC)
                term = jnp.dot(
                    rows[i, h, :, :, :, cols].reshape(FLAT, KC),
                    wgu[h, cols, :],
                    preferred_element_type=F32,
                )
                acc[...] = term if (h, c) == (0, 0) else acc[...] + term

    def grad_hidden():
        for h in range(2):
            for c in range(2):
                cols = pl.ds(c * KC, KC)
                term = contract_last(
                    rows[GRAD, h, :, :, :, cols].reshape(FLAT, KC), wd[h, :, cols]
                )
                gh[...] = term if (h, c) == (0, 0) else gh[...] + term

    def silu(v):
        return v * jax.nn.sigmoid(v)

    NC = C // 3 if C % 384 == 0 else C

    def partial(j, h, c):
        for n in range(C // NC):
            if j == OUT:
                term = jnp.dot(
                    act[:, pl.ds(0, FFD)],
                    wd[h, :, pl.ds(c * C + n * NC, NC)],
                    preferred_element_type=F32,
                )
            else:
                term = contract_last(act[...], wgu[h, pl.ds(c * C + n * NC, NC), :])
            part[j, h, c, :, :, :, pl.ds(n * NC, NC)] = term.astype(BF16).reshape(
                SIDE, SIDE, PAIR, NC
            )

    def reduction(j):
        def sems(m):
            return r_send.at[j, m], r_recv.at[j, m]

        copies = {}
        for c in range(2):
            copies["sib", c] = remote(part.at[j, 1, c], sib_part.at[j, c], *sems(c), SIB)
        for m, tensor in enumerate((B_UP, B_DN, B_DN, B_UP, B_UP, B_DN)):
            copies["b", m] = remote(b_out.at[j, m], b_in.at[j, m], *sems(2 + m), tensor)
        for m, tensor in enumerate((A_UP, A_DN, A_DN, A_UP, A_UP, A_DN)):
            copies["a", m] = remote(a_out.at[j, m], a_in.at[j, m], *sems(8 + m), tensor)
        copies["end"] = remote(final.at[j, :, own], final.at[j, :, own], *sems(14), SIB)
        return copies

    r = [reduction(j) for j in range(2)]

    def chip_sum(j, line, c, place):
        return part[j, 0, c, line, place].astype(F32) + sib_part[j, c, place, line].astype(F32)

    def send_b(j, m, line, c, plus=None):
        for place in range(SIDE):
            value = chip_sum(j, line, c, place)
            if plus is not None:
                value = value + b_in[j, plus, place].astype(F32)
            b_out[j, m, place] = value.astype(BF16)
        go(r[j]["b", m])

    def s1(j, c):
        go(r[j]["sib", c])

    def s2(j):
        r[j]["sib", 0].wait_recv()
        send_b(j, 0, b_op, 0)
        r[j]["sib", 1].wait_recv()
        send_b(j, 1, b_op, 1)
        send_b(j, 2, b_dn, 0)
        send_b(j, 3, b_up, 1)

    def s4(j):
        r[j]["b", 0].wait_recv()
        send_b(j, 4, b_up, 0, plus=0)
        r[j]["b", 1].wait_recv()
        send_b(j, 5, b_dn, 1, plus=1)

    def send_a(j, m, place, c, plus=None):
        value = w_sum[j, c, place]
        if plus is not None:
            value = value + a_in[j, plus].astype(F32)
        a_out[j, m] = value.astype(BF16)
        go(r[j]["a", m])

    def s5(j):
        for c, (one, two) in enumerate(((2, 4), (3, 5))):
            r[j]["b", one].wait_recv()
            r[j]["b", two].wait_recv()
            for place in range(SIDE):
                w_sum[j, c, place] = (
                    chip_sum(j, b, c, place)
                    + b_in[j, one, place].astype(F32)
                    + b_in[j, two, place].astype(F32)
                )
            if c == 0:
                send_a(j, 0, a_op, 0)
                send_a(j, 2, a_dn, 0)
            else:
                send_a(j, 1, a_op, 1)
                send_a(j, 3, a_up, 1)

    def s7(j):
        r[j]["a", 0].wait_recv()
        send_a(j, 4, a_up, 0, plus=0)
        r[j]["a", 1].wait_recv()
        send_a(j, 5, a_dn, 1, plus=1)

    def s8(j):
        for c, (one, two) in enumerate(((2, 4), (3, 5))):
            r[j]["a", one].wait_recv()
            r[j]["a", two].wait_recv()
            value = (
                w_sum[j, c, a] + a_in[j, one].astype(F32) + a_in[j, two].astype(F32)
            )
            final[j, :, pl.ds(pl.multiple_of(core * H + c * C, C), C)] = value.astype(BF16)
        go(r[j]["end"])

    normed_tile(BWD, saved_v, 1)
    e0(BWD)
    for copy in load_gu + load_d:
        copy.start()
    e1(BWD)

    def inverse_of(k, total):
        z = saved_v[:, lanes(k)].astype(F32)
        return total + jnp.sum(z * z, axis=1, keepdims=True)

    total = lax.fori_loop(0, D // LANES, inverse_of, jnp.zeros((TOKD, 1), F32))
    inverse_v[...] = jnp.broadcast_to(lax.rsqrt(total * (1.0 / D) + EPS), inverse_v.shape)
    e2(BWD)
    e3(BWD)

    @pl.when(section != n_pipe - 1)
    def _():
        send_grad.wait_recv()

    @pl.when(section == n_pipe - 1)
    def _():
        load_loss.wait()

    grad_tile(GRAD, grad_v, 1)
    e0(GRAD)
    e4(BWD)
    e1(GRAD)

    @pl.when(section != 0)
    def _():
        send_fwd.wait_recv()

    @pl.when(section == 0)
    def _():
        load_fresh.wait()

    normed_tile(FWD, fwd_v, 0)
    e0(FWD)
    e2(GRAD)
    e5(BWD)
    e3(GRAD)
    e1(FWD)
    e6(BWD)
    for copy in load_gu:
        copy.wait()
    gate_up(BWD)
    e2(FWD)
    e4(GRAD)
    e3(FWD)
    e5(GRAD)
    e6(GRAD)
    for copy in load_d:
        copy.wait()
    grad_hidden()
    gate = acc[:, pl.ds(0, FFD)]
    sigma = jax.nn.sigmoid(gate)
    act[:, pl.ds(0, FFD)] = (
        gh[...] * acc[:, pl.ds(FFD, FFD)] * sigma * (1.0 + gate * (1.0 - sigma))
    ).astype(BF16)
    act[:, pl.ds(FFD, FFD)] = (gh[...] * (gate * sigma)).astype(BF16)
    partial(ROWG, 1, 0)
    s1(ROWG, 0)
    partial(ROWG, 1, 1)
    s1(ROWG, 1)
    e4(FWD)
    partial(ROWG, 0, 0)
    partial(ROWG, 0, 1)
    e5(FWD)
    s2(ROWG)
    e6(FWD)
    gate_up(FWD)
    act[:, pl.ds(0, FFD)] = (silu(acc[:, pl.ds(0, FFD)]) * acc[:, pl.ds(FFD, FFD)]).astype(BF16)
    s4(ROWG)
    partial(OUT, 1, 0)
    s1(OUT, 0)
    partial(OUT, 1, 1)
    s1(OUT, 1)
    partial(OUT, 0, 0)
    partial(OUT, 0, 1)
    s2(OUT)
    s5(ROWG)
    s4(OUT)
    s7(ROWG)
    s8(ROWG)
    s5(OUT)

    r[ROWG]["end"].wait_recv()
    pick_bwd = token_pick(1)

    def project(k, total):
        adjusted = (
            jnp.dot(pick_bwd, final[ROWG, :, lanes(k)], preferred_element_type=F32)
            * gain_v[:, lanes(k)]
        )
        return total + jnp.sum(
            adjusted * saved_v[:, lanes(k)].astype(F32), axis=1, keepdims=True
        )

    total = lax.fori_loop(0, D // LANES, project, jnp.zeros((TOKD, 1), F32))
    inverse = inverse_v[:, pl.ds(0, 1)]
    factor = (inverse * inverse * inverse) * (total * (1.0 / D))

    def finish_grad(k, carry):
        adjusted = (
            jnp.dot(pick_bwd, final[ROWG, :, lanes(k)], preferred_element_type=F32)
            * gain_v[:, lanes(k)]
        )
        og_v[:, lanes(k)] = (
            grad_v[:, lanes(k)].astype(F32)
            + adjusted * inverse
            - saved_v[:, lanes(k)].astype(F32) * factor
        ).astype(BF16)
        return carry

    s7(OUT)
    lax.fori_loop(0, D // LANES, finish_grad, 0)
    store_grad.start()

    s8(OUT)
    pick_fwd = token_pick(0)
    scale = column(weight_v[pl.ds(0, 1), :])
    r[OUT]["end"].wait_recv()

    def finish_fwd(k, carry):
        spread = jnp.dot(pick_fwd, final[OUT, :, lanes(k)], preferred_element_type=F32)
        of_v[:, lanes(k)] = (fwd_v[:, lanes(k)].astype(F32) + scale * spread).astype(BF16)
        return carry

    lax.fori_loop(0, D // LANES, finish_fwd, 0)
    store_fwd.start()
    for copy in sent:
        copy.wait_send()

    @pl.when(section != n_pipe - 1)
    def _():
        send_fwd.wait_send()

    @pl.when(section != 0)
    def _():
        send_grad.wait_send()

    store_grad.wait()
    store_fwd.wait()


def on_device(
    n_pipe,
    fresh_batch,
    handed_forward,
    saved_inputs,
    handed_grads,
    loss_grad,
    norm_gain,
    route_slot,
    route_weight,
    w_gate,
    w_up,
    w_down,
):
    TOKD, D = fresh_batch.shape
    FFD = w_down.shape[1]
    H, C = D // 2, D // 4
    FLAT = SIDE * SIDE * PAIR
    anywhere = pl.BlockSpec(memory_space=pl.ANY)
    vmem = pltpu.VMEM
    dma = pltpu.SemaphoreType.DMA
    shape = jax.ShapeDtypeStruct((1, TOKD, D), BF16)
    return pl.pallas_call(
        functools.partial(kernel, n_pipe),
        out_shape=(shape, shape),
        in_specs=[anywhere] * 11,
        out_specs=(anywhere, anywhere),
        scratch_shapes=[
            vmem((TOKD, D), BF16),
            vmem((TOKD, D), BF16),
            vmem((TOKD, D), BF16),
            vmem((1, D), F32),
            vmem((2, TOKD), jnp.int32),
            vmem((2, TOKD), F32),
            vmem((2, H, 2 * FFD), BF16),
            vmem((2, FFD, H), BF16),
            vmem((PAIR, D), F32),
            vmem((3, PAIR, D), BF16),
            vmem((3, PAIR, H), BF16),
            vmem((3, 2, SIDE, SIDE, PAIR, H), BF16),
            vmem((FLAT, 2 * FFD), F32),
            vmem((FLAT, FFD), F32),
            vmem((FLAT, 2 * FFD), BF16),
            vmem((2, 2, 2, SIDE, SIDE, PAIR, C), BF16),
            vmem((2, 2, SIDE, SIDE, PAIR, C), BF16),
            vmem((2, 6, SIDE, PAIR, C), BF16),
            vmem((2, 6, SIDE, PAIR, C), BF16),
            vmem((2, 2, SIDE, PAIR, C), F32),
            vmem((2, 6, PAIR, C), BF16),
            vmem((2, 6, PAIR, C), BF16),
            vmem((2, PAIR, D), BF16),
            vmem((TOKD, 128), F32),
            vmem((TOKD, D), BF16),
            vmem((TOKD, D), BF16),
            dma((14,)),
            dma((2,)),
            dma((2,)),
            dma((3, 13)),
            dma((3, 13)),
            dma((2, 15)),
            dma((2, 15)),
        ],
        compiler_params=pltpu.CompilerParams(
            collective_id=0, has_side_effects=True, vmem_limit_bytes=56 * 2**20
        ),
    )(
        fresh_batch,
        handed_forward,
        saved_inputs,
        handed_grads,
        loss_grad,
        norm_gain,
        route_slot,
        route_weight,
        w_gate,
        w_up,
        w_down,
    )


def solution(mesh):
    placed = (
        P("tensor", None),
        P("pipe", "tensor", None),
        P("pipe", "tensor", None),
        P("pipe", "tensor", None),
        P("tensor", None),
        P("pipe", None),
        P("pipe", None, "tensor"),
        P("pipe", None, "tensor"),
        P("pipe", None, "tensor"),
        P("pipe", None, "tensor"),
        P("pipe", "tensor", None),
    )
    return jax.shard_map(
        functools.partial(on_device, mesh.shape["pipe"]),
        mesh=mesh,
        in_specs=placed,
        out_specs=(P("pipe", "tensor", None), P("pipe", "tensor", None)),
        check_vma=False,
    )
```

```python
import functools

import jax
import jax.numpy as jnp
from jax import lax
from jax.experimental import pallas as pl
from jax.experimental.pallas import tpu as pltpu
from jax.sharding import PartitionSpec as P

LCAP = 8
SIDE = 4
PAIR = 2 * LCAP
EPS = 1e-05
F32 = jnp.float32
BF16 = jnp.bfloat16
BWD, GRAD, FWD = 0, 1, 2
ROWG, OUT = 0, 1


def contract_last(left, right):
    return lax.dot_general(left, right, (((1,), (1,)), ((), ())), preferred_element_type=F32)
ORDER = (
    ("own", 0), ("weights_gu",), ("own_b", 0), ("pair", 0), ("fd", 0, 0), ("opposite", 0),
    ("fu", 0, 1), ("tile", 1), ("fd", 0, 1), ("fu", 0, 0), ("fd", 0, 2), ("own", 1),
    ("fu", 0, 2), ("tile", 2), ("own_b", 1), ("last_pair", 0), ("own", 2), ("last", 0),
    ("pair", 1), ("opposite", 1), ("gu", 0, 0), ("fd", 1, 0), ("fu", 1, 0), ("weights_d",),
    ("own_b", 2), ("fd", 1, 1), ("fu", 1, 1), ("fd", 1, 2), ("fu", 1, 2), ("pair", 2),
    ("handed", 0), ("opposite", 2), ("fu", 2, 0), ("fd", 2, 0), ("gu", 0, 1), ("last_pair", 1),
    ("last", 1), ("gh", 0), ("handed", 1), ("gh", 1), ("act_rowg",), ("fu", 2, 1), ("fd", 2, 1),
    ("p0", 0, 0), ("fd", 2, 2), ("fu", 2, 2), ("p1", 0, 1), ("p1", 0, 0), ("p0", 0, 1),
    ("m1", 0), ("last_pair", 2), ("m3", 0), ("last", 2), ("gu", 2, 0), ("m0", 0), ("m2", 0),
    ("handed", 2), ("gu", 2, 1), ("act_out",), ("p1", 1, 0), ("p1", 1, 1), ("p0", 1, 0),
    ("m0", 1), ("m5", 0), ("p0", 1, 1), ("m3", 1), ("m1", 1), ("m2", 1), ("m4", 0), ("m4", 1),
    ("m5", 1), ("w", 0, 0), ("w", 0, 1), ("w", 1, 0), ("w", 1, 1), ("x", 0, 0), ("x", 0, 1),
    ("x", 1, 0), ("ended", 0), ("project",), ("x", 1, 1), ("finish_fwd", 0), ("finish_grad",),
    ("ended", 1), ("finish_fwd", 1),
)


def kernel(
    n_pipe,
    fresh,
    handed_fwd,
    saved,
    handed_grads,
    loss_grad,
    gain,
    slot,
    weight,
    w_gate,
    w_up,
    w_down,
    out_fwd,
    out_grad,
    saved_v,
    fwd_v,
    grad_v,
    gain_v,
    slot_v,
    weight_v,
    wgu,
    wd,
    picked,
    tile,
    sib_tile,
    rows,
    acc,
    gh,
    act,
    part,
    sib_part,
    b_out,
    b_in,
    w_sum,
    a_out,
    a_in,
    final,
    inverse_v,
    changes,
    loc_sem,
    z_send,
    z_recv,
    g_send,
    g_recv,
    r_send,
    r_recv,
):
    D = saved.shape[2]
    TOKD = saved.shape[1]
    FFD = w_down.shape[1]
    H = D // 2
    C = D // 4
    LANES = min(1024, H)

    section = lax.axis_index("pipe")
    t = lax.axis_index("tensor")
    core = t % 2
    x = t // (2 * SIDE)
    y = (t // 2) % SIDE
    a = x + core * (y - x)
    b = y + core * (x - y)
    sa = 2 * SIDE - core * (2 * SIDE - 2)
    sb = 2 + core * (2 * SIDE - 2)
    A_UP = ((a + 1) % SIDE) * sa + b * sb + core
    A_OP = ((a + 2) % SIDE) * sa + b * sb + core
    A_DN = ((a + 3) % SIDE) * sa + b * sb + core
    B_UP = a * sa + ((b + 1) % SIDE) * sb + core
    B_DN = a * sa + ((b + 3) % SIDE) * sb + core
    SIB = t + 1 - 2 * core
    Z_UP = (section + 1) % n_pipe
    Z_DN = (section + n_pipe - 1) % n_pipe
    own_cols = pl.ds(pl.multiple_of(core * H, H), H)
    oth = pl.ds(pl.multiple_of((1 - core) * H, H), H)

    def at(tensor):
        return {"pipe": section, "tensor": tensor}

    def local(src, dst, k):
        return pltpu.make_async_copy(src, dst, loc_sem.at[k])

    first = [
        local(saved.at[0], saved_v, 0),
        local(gain, gain_v, 1),
        local(slot.at[0], slot_v, 2),
        local(weight.at[0], weight_v, 3),
    ]
    load_gu = [
        local(w_gate.at[0, own_cols], wgu.at[0, :, pl.ds(0, FFD)], 4),
        local(w_gate.at[0, oth], wgu.at[1, :, pl.ds(0, FFD)], 5),
        local(w_up.at[0, own_cols], wgu.at[0, :, pl.ds(FFD, FFD)], 6),
        local(w_up.at[0, oth], wgu.at[1, :, pl.ds(FFD, FFD)], 7),
    ]
    load_d = [
        local(w_down.at[0, :, own_cols], wd.at[0], 8),
        local(w_down.at[0, :, oth], wd.at[1], 9),
    ]
    load_fresh = local(fresh, fwd_v, 10)
    load_loss = local(loss_grad, grad_v, 11)
    for copy in first:
        copy.start()

    barrier = pltpu.get_barrier_semaphore()
    for tensor in (SIB, A_UP, A_OP, A_DN, B_UP, B_DN):
        pl.semaphore_signal(
            barrier, inc=1, device_id=at(tensor), device_id_type=pl.DeviceIdType.MESH
        )
    for pipe in (Z_UP, Z_DN):
        pl.semaphore_signal(
            barrier,
            inc=1,
            device_id={"pipe": pipe, "tensor": t},
            device_id_type=pl.DeviceIdType.MESH,
        )
    sent = []

    def remote(src, dst, send_sem, recv_sem, tensor):
        copy = pltpu.make_async_remote_copy(
            src_ref=src,
            dst_ref=dst,
            send_sem=send_sem,
            recv_sem=recv_sem,
            device_id=at(tensor),
            device_id_type=pl.DeviceIdType.MESH,
        )
        return copy

    def go(copy):
        copy.start()
        sent.append(copy)
        return copy

    for copy in first:
        copy.wait()

    def row_pick(micro):
        places = lax.broadcasted_iota(jnp.int32, (PAIR, TOKD), 0) - core * LCAP
        slots = jnp.broadcast_to(slot_v[pl.ds(micro, 1), :], (PAIR, TOKD))
        return jnp.where((places == slots) & (places >= 0) & (places < LCAP), 1.0, 0.0)

    def column(row):
        wide = jnp.broadcast_to(row, (TOKD, TOKD))
        eye = lax.broadcasted_iota(jnp.int32, (TOKD, TOKD), 0) == lax.broadcasted_iota(
            jnp.int32, (TOKD, TOKD), 1
        )
        return jnp.sum(jnp.where(eye, wide, 0.0), axis=1, keepdims=True)

    def token_pick(micro):
        slots = column(slot_v[pl.ds(micro, 1), :].astype(F32))
        slots = jnp.broadcast_to(slots, (TOKD, PAIR))
        places = (
            lax.broadcasted_iota(jnp.int32, (TOKD, PAIR), 1) - core * LCAP
        ).astype(F32)
        return jnp.where(
            (places == slots) & (places >= 0.0) & (places < float(LCAP)), 1.0, 0.0
        ).astype(BF16)

    def lanes(k):
        return pl.ds(k * LANES, LANES)

    def normed_tile(i, source, micro):
        pick = row_pick(micro).astype(BF16)
        place = 0 if i == BWD else 1
        total = jnp.zeros((PAIR, 1), F32)
        for k in range(D // LANES):
            z = jnp.dot(pick, source[:, lanes(k)], preferred_element_type=F32)
            picked[place, :, lanes(k)] = z
            total = total + jnp.sum(z * z, axis=1, keepdims=True)
        inverse = lax.rsqrt(total * (1.0 / D) + EPS)
        for k in range(D // LANES):
            tile[i, :, lanes(k)] = (
                picked[place, :, lanes(k)] * inverse * gain_v[:, lanes(k)]
            ).astype(BF16)
        return inverse

    def grad_tile(i, source, micro):
        pick_f = row_pick(micro)
        pick = pick_f.astype(BF16)
        weights = jnp.sum(
            pick_f * jnp.broadcast_to(weight_v[pl.ds(micro, 1), :], (PAIR, TOKD)),
            axis=1,
            keepdims=True,
        )

        for k in range(D // LANES):
            g = jnp.dot(pick, source[:, lanes(k)], preferred_element_type=F32)
            tile[i, :, lanes(k)] = (weights * g).astype(BF16)

    C0, C1 = pl.ds(0, C), pl.ds(C, C)
    PAIR_OF = pl.ds(1, 2)

    def gather(i):
        count = iter(range(21))

        def send(src, dst, tensor):
            m = next(count)
            return remote(src, dst, g_send.at[i, m], g_recv.at[i, m], tensor)

        mine = rows.at[i, 0]
        copies = {
            "tile": send(tile.at[i, :, oth], sib_tile.at[i], SIB),
            "au": send(mine.at[0, 0], mine.at[0, 2], A_UP),
            "ad": send(mine.at[0, 0], mine.at[0, 1], A_DN),
            "ax": send(mine.at[0, 0], mine.at[0, 3], A_OP),
        }
        for k, group in enumerate((pl.ds(0, 1), PAIR_OF, pl.ds(3, 1))):
            copies["bu", k] = send(mine.at[0, group], mine.at[2, group], B_UP)
            copies["bd", k] = send(mine.at[0, group], mine.at[1, group], B_DN)
            copies["bu2", k] = send(
                mine.at[2, group, :, C0], mine.at[3, group, :, C0], B_UP
            )
            copies["bd2", k] = send(
                mine.at[1, group, :, C1], mine.at[3, group, :, C1], B_DN
            )
        for line in range(3):
            copies["s", line] = send(mine.at[line], rows.at[i, 1, :, line], SIB)
        first = pl.ds(0, 3)
        copies["s", 3] = send(mine.at[3, first], rows.at[i, 1, first, 3], SIB)
        copies["s", 4] = send(mine.at[3, 3], rows.at[i, 1, 3, 3], SIB)
        return copies

    g = [gather(i) for i in range(3)]

    def reduction(j):
        count = iter(range(20))

        def send(src, dst, tensor):
            m = next(count)
            return remote(src, dst, r_send.at[j, m], r_recv.at[j, m], tensor)

        copies = {}
        for k, lines in enumerate((pl.ds(3, 1), PAIR_OF, pl.ds(0, 1))):
            for c in range(2):
                copies["sib", k, c] = send(
                    part.at[j, 1, c, lines], sib_part.at[j, c, lines], SIB
                )
        for m, tensor in enumerate((B_UP, B_DN, B_DN, B_UP, B_UP, B_DN)):
            copies["b", m] = send(b_out.at[j, m], b_in.at[j, m], tensor)
        for c in range(2):
            for m, tensor in enumerate((A_UP, A_DN, A_OP)):
                copies["a", c, m] = send(a_out.at[j, c, m], a_in.at[j, c, m], tensor)
            cols = pl.ds(pl.multiple_of(core * H + c * C, C), C)
            copies["end", c] = send(final.at[j, :, cols], final.at[j, :, cols], SIB)
        return copies

    r = [reduction(j) for j in range(2)]

    def arrive(copy):
        copy.wait_recv()

    KC = C
    FLAT = SIDE * SIDE * PAIR

    def accumulate(dst, i, h, product):
        for c in range(2):
            cols = pl.ds(c * KC, KC)
            term = product(rows[i, h, :, :, :, cols].reshape(FLAT, KC), h, cols)
            dst[...] = term if (h, c) == (0, 0) else dst[...] + term

    def by_gate_up(left, h, cols):
        return jnp.dot(left, wgu[h, cols, :], preferred_element_type=F32)

    def by_down(left, h, cols):
        return contract_last(left, wd[h, :, cols])

    def gate_up(i, h):
        accumulate(acc.at[0 if i == BWD else 1], i, h, by_gate_up)

    def grad_hidden(h):
        accumulate(gh, GRAD, h, by_down)

    GATE, UP = pl.ds(0, FFD), pl.ds(FFD, FFD)

    def act_rowg():
        gate = acc[0, :, GATE]
        sigma = jax.nn.sigmoid(gate)
        grad = gh[...]
        act[0, :, GATE] = (
            grad * acc[0, :, UP] * sigma * (1.0 + gate * (1.0 - sigma))
        ).astype(BF16)
        act[0, :, UP] = (grad * (gate * sigma)).astype(BF16)

    def act_out():
        gate = acc[1, :, GATE]
        act[1, :, GATE] = (gate * jax.nn.sigmoid(gate) * acc[1, :, UP]).astype(BF16)

    NC = C // 3 if C % 384 == 0 else C

    def partial(j, h, c):
        for n in range(C // NC):
            if j == OUT:
                term = jnp.dot(
                    act[1, :, GATE],
                    wd[h, :, pl.ds(c * C + n * NC, NC)],
                    preferred_element_type=F32,
                )
            else:
                term = contract_last(act[0], wgu[h, pl.ds(c * C + n * NC, NC), :])
            term = term.astype(BF16).reshape(SIDE, SIDE, PAIR, NC)
            cols = pl.ds(n * NC, NC)
            if h == 0:
                part[j, 0, c, :, :, :, cols] = term
            else:
                for line in range(SIDE):
                    part[j, 1, c, line, :, :, cols] = term[:, line]

    def chip_sum(j, line, c):
        return part[j, 0, c, line].astype(F32) + sib_part[j, c, line].astype(F32)

    def send_b(j, m, line, c, plus=None):
        value = chip_sum(j, line, c)
        if plus is not None:
            value = value + b_in[j, plus].astype(F32)
        b_out[j, m] = value.astype(BF16)
        go(r[j]["b", m])

    def line_sum(j, c):
        one, two = 2 + c, 4 + c
        arrive(r[j]["b", one])
        arrive(r[j]["b", two])
        total = chip_sum(j, 0, c) + b_in[j, one].astype(F32) + b_in[j, two].astype(F32)
        a_out[j, c] = total[1:].astype(BF16)
        w_sum[j, c] = total[0]
        for m in range(3):
            go(r[j]["a", c, m])

    def block_sum(j, c):
        total = w_sum[j, c]
        for m in range(3):
            arrive(r[j]["a", c, m])
            total = total + a_in[j, c, m].astype(F32)
        final[j, :, pl.ds(pl.multiple_of(core * H + c * C, C), C)] = total.astype(BF16)
        go(r[j]["end", c])

    def half_lanes(h, k):
        start = (core if h == 0 else 1 - core) * H
        return pl.ds(pl.multiple_of(start + k * LANES, LANES), LANES)

    def project():
        inverse = inverse_v[:, pl.ds(0, 1)]
        total = jnp.zeros((PAIR, 1), F32)
        for k in range(D // LANES):
            adjusted = final[ROWG, :, lanes(k)].astype(F32) * gain_v[:, lanes(k)]
            total = total + jnp.sum(adjusted * picked[0, :, lanes(k)], axis=1, keepdims=True)
        factor = (inverse * inverse * inverse) * (total * (1.0 / D))
        for k in range(D // LANES):
            adjusted = final[ROWG, :, lanes(k)].astype(F32) * gain_v[:, lanes(k)]
            change = adjusted * inverse - picked[0, :, lanes(k)] * factor
            high = change.astype(BF16)
            changes[0, :, lanes(k)] = high
            changes[1, :, lanes(k)] = (change - high.astype(F32)).astype(BF16)

    def finish_grad():
        pick = token_pick(1)
        for k in range(D // LANES):
            cols = lanes(k)
            out_grad[0, :, cols] = (
                grad_v[:, cols].astype(F32)
                + jnp.dot(pick, changes[0, :, cols], preferred_element_type=F32)
                + jnp.dot(pick, changes[1, :, cols], preferred_element_type=F32)
            ).astype(BF16)

    def finish_fwd(h):
        pick = token_pick(0)
        scale = column(weight_v[pl.ds(0, 1), :])

        for k in range(H // LANES):
            cols = half_lanes(h, k)
            spread = jnp.dot(pick, final[OUT, :, cols], preferred_element_type=F32)
            out_fwd[0, :, cols] = (fwd_v[:, cols].astype(F32) + scale * spread).astype(BF16)

    def tile_of(i):
        if i == GRAD:

            @pl.when(section != n_pipe - 1)
            def _():
                send_grad.wait_recv()

            @pl.when(section == n_pipe - 1)
            def _():
                load_loss.wait()

            grad_tile(GRAD, grad_v, 1)
        elif i == FWD:

            @pl.when(section != 0)
            def _():
                send_fwd.wait_recv()

            @pl.when(section == 0)
            def _():
                load_fresh.wait()

            normed_tile(FWD, fwd_v, 0)
        go(g[i]["tile"])

    def own(i):
        arrive(g[i]["tile"])
        rows[i, 0, 0, 0] = tile[i, :, own_cols] + sib_tile[i]
        for name in ("au", "ad", "ax"):
            go(g[i][name])

    def own_b(i):
        go(g[i]["bu", 0])
        go(g[i]["bd", 0])

    def pair(i):
        arrive(g[i]["au"])
        arrive(g[i]["ad"])
        go(g[i]["bu", 1])
        go(g[i]["bd", 1])

    def opposite(i):
        arrive(g[i]["ax"])
        go(g[i]["bu", 2])
        go(g[i]["bd", 2])
        go(g[i]["s", 0])

    def forward_up(i, k):
        arrive(g[i]["bu", k])
        go(g[i]["bu2", k])
        if k == 2:
            go(g[i]["s", 2])

    def forward_dn(i, k):
        arrive(g[i]["bd", k])
        go(g[i]["bd2", k])
        if k == 2:
            go(g[i]["s", 1])

    def last_pair(i):
        for k in range(2):
            arrive(g[i]["bu2", k])
            arrive(g[i]["bd2", k])
        go(g[i]["s", 3])

    def last(i):
        arrive(g[i]["bu2", 2])
        arrive(g[i]["bd2", 2])
        go(g[i]["s", 4])

    def handed(i):
        for line in range(5):
            arrive(g[i]["s", line])

    def weights_gu():
        for copy in load_gu:
            copy.wait()

    def weights_d():
        for copy in load_d:
            copy.wait()

    def p1(j, c):
        partial(j, 1, c)
        for k in range(3):
            go(r[j]["sib", k, c])

    def p0(j, c):
        partial(j, 0, c)

    def m0(j):
        arrive(r[j]["sib", 0, 0])
        send_b(j, 0, 3, 0)

    def m1(j):
        arrive(r[j]["sib", 0, 1])
        send_b(j, 1, 3, 1)

    def m2(j):
        arrive(r[j]["sib", 1, 0])
        send_b(j, 2, 2, 0)

    def m3(j):
        arrive(r[j]["sib", 1, 1])
        send_b(j, 3, 1, 1)

    def m4(j):
        arrive(r[j]["b", 0])
        send_b(j, 4, 1, 0, plus=0)

    def m5(j):
        arrive(r[j]["b", 1])
        send_b(j, 5, 2, 1, plus=1)

    def w(j, c):
        arrive(r[j]["sib", 2, c])
        line_sum(j, c)

    def ended(j):
        for c in range(2):
            arrive(r[j]["end", c])

    tasks = dict(
        tile=tile_of,
        own=own,
        own_b=own_b,
        pair=pair,
        opposite=opposite,
        fu=forward_up,
        fd=forward_dn,
        last_pair=last_pair,
        last=last,
        handed=handed,
        gu=gate_up,
        gh=grad_hidden,
        act_rowg=act_rowg,
        act_out=act_out,
        p1=p1,
        p0=p0,
        m0=m0,
        m1=m1,
        m2=m2,
        m3=m3,
        m4=m4,
        m5=m5,
        w=w,
        x=block_sum,
        ended=ended,
        project=project,
        finish_grad=finish_grad,
        finish_fwd=finish_fwd,
        weights_gu=weights_gu,
        weights_d=weights_d,
    )

    inverse = normed_tile(BWD, saved_v, 1)
    inverse_v[...] = jnp.broadcast_to(inverse, inverse_v.shape)
    pl.semaphore_wait(barrier, 8)

    send_fwd = pltpu.make_async_remote_copy(
        src_ref=handed_fwd.at[0],
        dst_ref=fwd_v,
        send_sem=z_send.at[0],
        recv_sem=z_recv.at[0],
        device_id={"pipe": Z_UP, "tensor": t},
        device_id_type=pl.DeviceIdType.MESH,
    )
    send_grad = pltpu.make_async_remote_copy(
        src_ref=handed_grads.at[0],
        dst_ref=grad_v,
        send_sem=z_send.at[1],
        recv_sem=z_recv.at[1],
        device_id={"pipe": Z_DN, "tensor": t},
        device_id_type=pl.DeviceIdType.MESH,
    )

    @pl.when(section != n_pipe - 1)
    def _():
        send_fwd.start()

    @pl.when(section != 0)
    def _():
        send_grad.start()

    @pl.when(section == 0)
    def _():
        load_fresh.start()

    @pl.when(section == n_pipe - 1)
    def _():
        load_loss.start()

    go(g[BWD]["tile"])
    for copy in load_gu + load_d:
        copy.start()
    for name, *at_ in ORDER:
        tasks[name](*at_)

    for copy in sent:
        copy.wait_send()

    @pl.when(section != n_pipe - 1)
    def _():
        send_fwd.wait_send()

    @pl.when(section != 0)
    def _():
        send_grad.wait_send()


def place(fwd_in, grad_in, fwd_out, grad_out, sem):
    copies = [
        pltpu.make_async_copy(fwd_in, fwd_out, sem.at[0]),
        pltpu.make_async_copy(grad_in, grad_out, sem.at[1]),
    ]
    for copy in copies:
        copy.start()
    for copy in copies:
        copy.wait()


def on_device(
    n_pipe,
    fresh_batch,
    handed_forward,
    saved_inputs,
    handed_grads,
    loss_grad,
    norm_gain,
    route_slot,
    route_weight,
    w_gate,
    w_up,
    w_down,
):
    TOKD, D = fresh_batch.shape
    FFD = w_down.shape[1]
    H, C = D // 2, D // 4
    FLAT = SIDE * SIDE * PAIR
    anywhere = pl.BlockSpec(memory_space=pl.ANY)
    vmem = pltpu.VMEM
    dma = pltpu.SemaphoreType.DMA
    shape = jax.ShapeDtypeStruct((1, TOKD, D), BF16)
    inside = vmem((1, TOKD, D), BF16)
    in_vmem = pl.BlockSpec(memory_space=vmem)
    results = pl.pallas_call(
        functools.partial(kernel, n_pipe),
        out_shape=(inside, inside),
        in_specs=[anywhere] * 11,
        out_specs=(in_vmem, in_vmem),
        scratch_shapes=[
            vmem((TOKD, D), BF16),
            vmem((TOKD, D), BF16),
            vmem((TOKD, D), BF16),
            vmem((1, D), F32),
            vmem((2, TOKD), jnp.int32),
            vmem((2, TOKD), F32),
            vmem((2, H, 2 * FFD), BF16),
            vmem((2, FFD, H), BF16),
            vmem((2, PAIR, D), F32),
            vmem((3, PAIR, D), BF16),
            vmem((3, PAIR, H), BF16),
            vmem((3, 2, SIDE, SIDE, PAIR, H), BF16),
            vmem((2, FLAT, 2 * FFD), F32),
            vmem((FLAT, FFD), F32),
            vmem((2, FLAT, 2 * FFD), BF16),
            vmem((2, 2, 2, SIDE, SIDE, PAIR, C), BF16),
            vmem((2, 2, SIDE, SIDE, PAIR, C), BF16),
            vmem((2, 6, SIDE, PAIR, C), BF16),
            vmem((2, 6, SIDE, PAIR, C), BF16),
            vmem((2, 2, PAIR, C), F32),
            vmem((2, 2, 3, PAIR, C), BF16),
            vmem((2, 2, 3, PAIR, C), BF16),
            vmem((2, PAIR, D), BF16),
            vmem((PAIR, 128), F32),
            vmem((2, PAIR, D), BF16),
            dma((12,)),
            dma((2,)),
            dma((2,)),
            dma((3, 21)),
            dma((3, 21)),
            dma((2, 20)),
            dma((2, 20)),
        ],
        compiler_params=pltpu.CompilerParams(
            collective_id=0, has_side_effects=True, vmem_limit_bytes=56 * 2**20
        ),
    )(
        fresh_batch,
        handed_forward,
        saved_inputs,
        handed_grads,
        loss_grad,
        norm_gain,
        route_slot,
        route_weight,
        w_gate,
        w_up,
        w_down,
    )
    return pl.pallas_call(
        place,
        out_shape=(shape, shape),
        in_specs=[in_vmem] * 2,
        out_specs=(anywhere, anywhere),
        scratch_shapes=[dma((2,))],
        compiler_params=pltpu.CompilerParams(vmem_limit_bytes=8 * 2**20),
    )(*results)


def solution(mesh):
    placed = (
        P("tensor", None),
        P("pipe", "tensor", None),
        P("pipe", "tensor", None),
        P("pipe", "tensor", None),
        P("tensor", None),
        P("pipe", None),
        P("pipe", None, "tensor"),
        P("pipe", None, "tensor"),
        P("pipe", None, "tensor"),
        P("pipe", None, "tensor"),
        P("pipe", "tensor", None),
    )
    return jax.shard_map(
        functools.partial(on_device, mesh.shape["pipe"]),
        mesh=mesh,
        in_specs=placed,
        out_specs=(P("pipe", "tensor", None), P("pipe", "tensor", None)),
        check_vma=False,
    )
```

```python
import functools

import jax
import jax.numpy as jnp
from jax import lax
from jax.experimental import pallas as pl
from jax.experimental.pallas import tpu as pltpu
from jax.sharding import PartitionSpec as P

LCAP = 8
SIDE = 4
PAIR = 2 * LCAP
EPS = 1e-05
F32 = jnp.float32
BF16 = jnp.bfloat16
BWD, GRAD, FWD = 0, 1, 2
FWD_WAY, GRAD_WAY = 0, 1
ROWG, OUT = 0, 1


def contract_last(left, right):
    return lax.dot_general(left, right, (((1,), (1,)), ((), ())), preferred_element_type=F32)
HOPS_G = (False, True, True)
HOPS_R = (True, False)
ORDER = (
    ("own", 0), ("pack", 1), ("pack", 2), ("own_b", 0), ("pair", 0), ("opposite", 0),
    ("weights_d",), ("tile", 1), ("fd", 0, 0), ("fu", 0, 0), ("own", 1), ("fd", 0, 1),
    ("fu", 0, 1), ("tile", 2), ("own_b", 1), ("own", 2), ("fa", 1), ("weights_gu",),
    ("pair", 1), ("last_pair", 0), ("fu", 0, 2), ("fa", 2), ("fd", 0, 2), ("opposite", 1),
    ("own_b", 2), ("fd", 1, 0), ("fu", 1, 0), ("fu", 1, 1), ("last", 0), ("fd", 1, 1),
    ("gu", 0, 0), ("fu", 1, 2), ("fd", 1, 2), ("pair", 2), ("opposite", 2), ("handed", 0),
    ("gu", 0, 1), ("fd", 2, 0), ("last_pair", 1), ("last", 1), ("fu", 2, 0), ("gh", 0),
    ("handed", 1), ("gh", 1), ("relay_all",), ("act_rowg",), ("p1", 0, 1), ("fd", 2, 1),
    ("fu", 2, 1), ("p1", 0, 0), ("fd", 2, 2), ("fu", 2, 2), ("p0", 0, 1), ("m1", 0),
    ("p0", 0, 0), ("m0", 0), ("m3", 0), ("m2", 0), ("last_pair", 2), ("last", 2), ("gu", 2, 0),
    ("handed", 2), ("gu", 2, 1), ("act_out",), ("m5", 0), ("p1", 1, 1), ("m4", 0), ("p0", 1, 1),
    ("p1", 1, 0), ("m1", 1), ("p0", 1, 0), ("m0", 1), ("m3", 1), ("m2", 1), ("w", 0, 1),
    ("m5", 1), ("w", 0, 0), ("m4", 1), ("v", 0, 0), ("v", 0, 1), ("w", 1, 1), ("w", 1, 0),
    ("x", 0, 0), ("x", 0, 1), ("ended", 0), ("project",), ("relayed", 1), ("finish_grad",),
    ("x", 1, 1), ("x", 1, 0), ("relayed", 2), ("finish_fwd", 0), ("ended", 1),
    ("finish_fwd", 1),
)


def kernel(
    n_pipe,
    fresh,
    handed_fwd,
    saved,
    handed_grads,
    loss_grad,
    gain,
    slot,
    weight,
    w_gate,
    w_up,
    w_down,
    out_fwd,
    out_grad,
    saved_v,
    fwd_v,
    grad_v,
    gain_v,
    slot_v,
    weight_v,
    source_v,
    slots_v,
    packed_out,
    packed_in,
    wgu,
    wd,
    picked,
    tile,
    sib_tile,
    rows,
    acc,
    gh,
    act,
    part,
    sib_part,
    b_out,
    b_in,
    w_sum,
    a_out,
    a_in,
    final,
    inverse_v,
    changes,
    loc_sem,
    z_send,
    z_recv,
    g_send,
    g_recv,
    r_send,
    r_recv,
):
    D = saved.shape[2]
    TOKD = saved.shape[1]
    FFD = w_down.shape[1]
    H = D // 2
    C = D // 4
    LANES = min(1024, H)

    section = lax.axis_index("pipe")
    t = lax.axis_index("tensor")
    core = t % 2
    x = t // (2 * SIDE)
    y = (t // 2) % SIDE
    a = x + core * (y - x)
    b = y + core * (x - y)
    sa = 2 * SIDE - core * (2 * SIDE - 2)
    sb = 2 + core * (2 * SIDE - 2)
    A_UP = ((a + 1) % SIDE) * sa + b * sb + core
    A_OP = ((a + 2) % SIDE) * sa + b * sb + core
    A_DN = ((a + 3) % SIDE) * sa + b * sb + core
    B_UP = a * sa + ((b + 1) % SIDE) * sb + core
    B_DN = a * sa + ((b + 3) % SIDE) * sb + core
    SIB = t + 1 - 2 * core
    Z_UP = (section + 1) % n_pipe
    Z_DN = (section + n_pipe - 1) % n_pipe
    own_cols = pl.ds(pl.multiple_of(core * H, H), H)
    oth = pl.ds(pl.multiple_of((1 - core) * H, H), H)

    def at(tensor):
        return {"pipe": section, "tensor": tensor}

    def local(src, dst, k):
        return pltpu.make_async_copy(src, dst, loc_sem.at[k])

    first = [
        local(saved.at[0], saved_v, 0),
        local(gain, gain_v, 1),
        local(slot.at[0], slot_v, 2),
        local(weight.at[0], weight_v, 3),
    ]
    load_gu = [
        local(w_gate.at[0, own_cols], wgu.at[0, :, pl.ds(0, FFD)], 4),
        local(w_gate.at[0, oth], wgu.at[1, :, pl.ds(0, FFD)], 5),
        local(w_up.at[0, own_cols], wgu.at[0, :, pl.ds(FFD, FFD)], 6),
        local(w_up.at[0, oth], wgu.at[1, :, pl.ds(FFD, FFD)], 7),
    ]
    load_d = [
        local(w_down.at[0, :, own_cols], wd.at[0], 8),
        local(w_down.at[0, :, oth], wd.at[1], 9),
    ]
    load_fresh = local(fresh, fwd_v, 10)
    load_loss = local(loss_grad, grad_v, 11)
    load_sources = [
        local(handed_fwd.at[0], source_v.at[FWD_WAY], 12),
        local(handed_grads.at[0], source_v.at[GRAD_WAY], 13),
    ]
    for copy in first + load_sources:
        copy.start()

    barrier = pltpu.get_barrier_semaphore()
    for tensor in (SIB, A_UP, A_OP, A_DN, B_UP, B_DN):
        pl.semaphore_signal(
            barrier, inc=1, device_id=at(tensor), device_id_type=pl.DeviceIdType.MESH
        )
    for pipe in (Z_UP, Z_DN):
        pl.semaphore_signal(
            barrier,
            inc=1,
            device_id={"pipe": pipe, "tensor": t},
            device_id_type=pl.DeviceIdType.MESH,
        )
    sent = []

    def remote(src, dst, send_sem, recv_sem, tensor):
        copy = pltpu.make_async_remote_copy(
            src_ref=src,
            dst_ref=dst,
            send_sem=send_sem,
            recv_sem=recv_sem,
            device_id=at(tensor),
            device_id_type=pl.DeviceIdType.MESH,
        )
        return copy

    def go(copy):
        copy.start()
        sent.append(copy)
        return copy

    for copy in first:
        copy.wait()

    def row_pick(micro):
        places = lax.broadcasted_iota(jnp.int32, (PAIR, TOKD), 0) - core * LCAP
        slots = jnp.broadcast_to(slot_v[pl.ds(micro, 1), :], (PAIR, TOKD))
        return jnp.where((places == slots) & (places >= 0) & (places < LCAP), 1.0, 0.0)

    def column(row):
        wide = jnp.broadcast_to(row, (TOKD, TOKD))
        eye = lax.broadcasted_iota(jnp.int32, (TOKD, TOKD), 0) == lax.broadcasted_iota(
            jnp.int32, (TOKD, TOKD), 1
        )
        return jnp.sum(jnp.where(eye, wide, 0.0), axis=1, keepdims=True)

    def token_pick(micro):
        slots = column(slot_v[pl.ds(micro, 1), :].astype(F32))
        slots = jnp.broadcast_to(slots, (TOKD, PAIR))
        places = (
            lax.broadcasted_iota(jnp.int32, (TOKD, PAIR), 1) - core * LCAP
        ).astype(F32)
        return jnp.where(
            (places == slots) & (places >= 0.0) & (places < float(LCAP)), 1.0, 0.0
        ).astype(BF16)

    def lanes(k):
        return pl.ds(k * LANES, LANES)

    def pack(source, slots):
        places = lax.broadcasted_iota(jnp.int32, (PAIR, TOKD), 0)
        slots = jnp.broadcast_to(slots, (PAIR, TOKD))
        low = jnp.where((places == slots) & (places < LCAP), 1.0, 0.0).astype(BF16)
        high = jnp.where((places - LCAP == slots) & (slots < LCAP), 1.0, 0.0).astype(BF16)
        parts = []
        for k in range(H // LANES):
            parts.append(
                jnp.dot(low, source[:, lanes(k)], preferred_element_type=F32)
                + jnp.dot(high, source[:, lanes(k + H // LANES)], preferred_element_type=F32)
            )
        return parts

    def store_pack(dst, parts):
        for k, value in enumerate(parts):
            dst[:, lanes(k)] = value.astype(BF16)

    def unpacked(way, k):
        half, k = k // (H // LANES), k % (H // LANES)
        places = lax.broadcasted_iota(jnp.int32, (PAIR, PAIR), 0) - core * LCAP
        origin = lax.broadcasted_iota(jnp.int32, (PAIR, PAIR), 1) - half * LCAP
        pick = jnp.where((places == origin) & (places >= 0) & (places < LCAP), 1.0, 0.0)
        return jnp.dot(
            pick.astype(BF16), packed_in[way, :, lanes(k)], preferred_element_type=F32
        )

    def normed_tile(i):
        pick = row_pick(1).astype(BF16)
        place = 0 if i == BWD else 1
        total = jnp.zeros((PAIR, 1), F32)
        for k in range(D // LANES):
            if i == BWD:
                z = jnp.dot(pick, saved_v[:, lanes(k)], preferred_element_type=F32)
            else:
                z = unpacked(FWD_WAY, k)
            picked[place, :, lanes(k)] = z
            total = total + jnp.sum(z * z, axis=1, keepdims=True)
        inverse = lax.rsqrt(total * (1.0 / D) + EPS)
        for k in range(D // LANES):
            tile[i, :, lanes(k)] = (
                picked[place, :, lanes(k)] * inverse * gain_v[:, lanes(k)]
            ).astype(BF16)
        return inverse

    def grad_tile():
        pick = row_pick(1)
        weights = jnp.sum(
            pick * jnp.broadcast_to(weight_v[pl.ds(1, 1), :], (PAIR, TOKD)),
            axis=1,
            keepdims=True,
        )
        for k in range(D // LANES):
            g = unpacked(GRAD_WAY, k)
            tile[GRAD, :, lanes(k)] = (weights * g).astype(BF16)

    C0, C1 = pl.ds(0, C), pl.ds(C, C)
    PAIR_OF = pl.ds(1, 2)

    def gather(i):
        count = iter(range(22))

        def send(src, dst, tensor):
            m = next(count)
            return remote(src, dst, g_send.at[i, m], g_recv.at[i, m], tensor)

        mine = rows.at[i, 0]
        copies = {
            "tile": send(tile.at[i, :, oth], sib_tile.at[i], SIB),
            "au": send(mine.at[0, 0], mine.at[0, 2], A_UP),
            "ad": send(mine.at[0, 0], mine.at[0, 1], A_DN),
        }
        if HOPS_G[i]:
            copies["au2"] = send(mine.at[0, 2, :, C0], mine.at[0, 3, :, C0], A_UP)
            copies["ad2"] = send(mine.at[0, 1, :, C1], mine.at[0, 3, :, C1], A_DN)
        else:
            copies["ax"] = send(mine.at[0, 0], mine.at[0, 3], A_OP)
        for k, group in enumerate((pl.ds(0, 1), PAIR_OF, pl.ds(3, 1))):
            copies["bu", k] = send(mine.at[0, group], mine.at[2, group], B_UP)
            copies["bd", k] = send(mine.at[0, group], mine.at[1, group], B_DN)
            copies["bu2", k] = send(
                mine.at[2, group, :, C0], mine.at[3, group, :, C0], B_UP
            )
            copies["bd2", k] = send(
                mine.at[1, group, :, C1], mine.at[3, group, :, C1], B_DN
            )
        for line in range(3):
            copies["s", line] = send(mine.at[line], rows.at[i, 1, :, line], SIB)
        first = pl.ds(0, 3)
        copies["s", 3] = send(mine.at[3, first], rows.at[i, 1, first, 3], SIB)
        copies["s", 4] = send(mine.at[3, 3], rows.at[i, 1, 3, 3], SIB)
        return copies

    g = [gather(i) for i in range(3)]

    def reduction(j):
        count = iter(range(20))

        def send(src, dst, tensor):
            m = next(count)
            return remote(src, dst, r_send.at[j, m], r_recv.at[j, m], tensor)

        copies = {}
        for k, lines in enumerate((pl.ds(3, 1), PAIR_OF, pl.ds(0, 1))):
            for c in range(2):
                copies["sib", k, c] = send(
                    part.at[j, 1, c, lines], sib_part.at[j, c, lines], SIB
                )
        for m, tensor in enumerate((B_UP, B_DN, B_DN, B_UP, B_UP, B_DN)):
            copies["b", m] = send(b_out.at[j, m], b_in.at[j, m], tensor)
        for c in range(2):
            far = (A_UP, A_DN)[c] if HOPS_R[j] else A_OP
            for m, tensor in enumerate((A_UP, A_DN, far)):
                copies["a", c, m] = send(a_out.at[j, c, m], a_in.at[j, c, m], tensor)
            cols = pl.ds(pl.multiple_of(core * H + c * C, C), C)
            copies["end", c] = send(final.at[j, :, cols], final.at[j, :, cols], SIB)
        return copies

    r = [reduction(j) for j in range(2)]

    def arrive(copy):
        copy.wait_recv()

    KC = C
    FLAT = SIDE * SIDE * PAIR

    def accumulate(dst, i, h, product):
        for c in range(2):
            cols = pl.ds(c * KC, KC)
            term = product(rows[i, h, :, :, :, cols].reshape(FLAT, KC), h, cols)
            dst[...] = term if (h, c) == (0, 0) else dst[...] + term

    def by_gate_up(left, h, cols):
        return jnp.dot(left, wgu[h, cols, :], preferred_element_type=F32)

    def by_down(left, h, cols):
        return contract_last(left, wd[h, :, cols])

    def gate_up(i, h):
        accumulate(acc.at[0 if i == BWD else 1], i, h, by_gate_up)

    def grad_hidden(h):
        accumulate(gh, GRAD, h, by_down)

    GATE, UP = pl.ds(0, FFD), pl.ds(FFD, FFD)

    def act_rowg():
        gate = acc[0, :, GATE]
        sigma = jax.nn.sigmoid(gate)
        grad = gh[...]
        act[0, :, GATE] = (
            grad * acc[0, :, UP] * sigma * (1.0 + gate * (1.0 - sigma))
        ).astype(BF16)
        act[0, :, UP] = (grad * (gate * sigma)).astype(BF16)

    def act_out():
        gate = acc[1, :, GATE]
        act[1, :, GATE] = (gate * jax.nn.sigmoid(gate) * acc[1, :, UP]).astype(BF16)

    NC = C // 3 if C % 384 == 0 else C

    def partial(j, h, c):
        for n in range(C // NC):
            if j == OUT:
                term = jnp.dot(
                    act[1, :, GATE],
                    wd[h, :, pl.ds(c * C + n * NC, NC)],
                    preferred_element_type=F32,
                )
            else:
                term = contract_last(act[0], wgu[h, pl.ds(c * C + n * NC, NC), :])
            term = term.astype(BF16).reshape(SIDE, SIDE, PAIR, NC)
            cols = pl.ds(n * NC, NC)
            if h == 0:
                part[j, 0, c, :, :, :, cols] = term
            else:
                for line in range(SIDE):
                    part[j, 1, c, line, :, :, cols] = term[:, line]

    def chip_sum(j, line, c):
        return part[j, 0, c, line].astype(F32) + sib_part[j, c, line].astype(F32)

    def send_b(j, m, line, c, plus=None):
        value = chip_sum(j, line, c)
        if plus is not None:
            value = value + b_in[j, plus].astype(F32)
        b_out[j, m] = value.astype(BF16)
        go(r[j]["b", m])

    def line_sum(j, c):
        one, two = 2 + c, 4 + c
        arrive(r[j]["b", one])
        arrive(r[j]["b", two])
        total = chip_sum(j, 0, c) + b_in[j, one].astype(F32) + b_in[j, two].astype(F32)
        w_sum[j, c, 0] = total[0]
        if HOPS_R[j]:
            w_sum[j, c, 1] = total[1 + c]
            a_out[j, c, 2] = total[3].astype(BF16)
            a_out[j, c, 1 - c] = total[2 - c].astype(BF16)
            go(r[j]["a", c, 2])
            go(r[j]["a", c, 1 - c])
        else:
            a_out[j, c] = total[1:].astype(BF16)
            for m in range(3):
                go(r[j]["a", c, m])

    def hop_r(j, c):
        arrive(r[j]["a", c, 2])
        a_out[j, c, c] = (w_sum[j, c, 1] + a_in[j, c, 2].astype(F32)).astype(BF16)
        go(r[j]["a", c, c])

    def block_sum(j, c):
        total = w_sum[j, c, 0]
        for m in range(2) if HOPS_R[j] else range(3):
            arrive(r[j]["a", c, m])
            total = total + a_in[j, c, m].astype(F32)
        final[j, :, pl.ds(pl.multiple_of(core * H + c * C, C), C)] = total.astype(BF16)
        go(r[j]["end", c])

    def half_lanes(h, k):
        start = (core if h == 0 else 1 - core) * H
        return pl.ds(pl.multiple_of(start + k * LANES, LANES), LANES)

    def project():
        inverse = inverse_v[:, pl.ds(0, 1)]
        total = jnp.zeros((PAIR, 1), F32)
        for k in range(D // LANES):
            adjusted = final[ROWG, :, lanes(k)].astype(F32) * gain_v[:, lanes(k)]
            total = total + jnp.sum(adjusted * picked[0, :, lanes(k)], axis=1, keepdims=True)
        factor = (inverse * inverse * inverse) * (total * (1.0 / D))
        for k in range(D // LANES):
            adjusted = final[ROWG, :, lanes(k)].astype(F32) * gain_v[:, lanes(k)]
            change = adjusted * inverse - picked[0, :, lanes(k)] * factor
            high = change.astype(BF16)
            changes[0, :, lanes(k)] = high
            changes[1, :, lanes(k)] = (change - high.astype(F32)).astype(BF16)

    def finish_grad():
        pick = token_pick(1)
        for k in range(D // LANES):
            cols = lanes(k)
            out_grad[0, :, cols] = (
                grad_v[:, cols].astype(F32)
                + jnp.dot(pick, changes[0, :, cols], preferred_element_type=F32)
                + jnp.dot(pick, changes[1, :, cols], preferred_element_type=F32)
            ).astype(BF16)

    def finish_fwd(h):
        pick = token_pick(0)
        scale = column(weight_v[pl.ds(0, 1), :])

        for k in range(H // LANES):
            cols = half_lanes(h, k)
            spread = jnp.dot(pick, final[OUT, :, cols], preferred_element_type=F32)
            out_fwd[0, :, cols] = (fwd_v[:, cols].astype(F32) + scale * spread).astype(BF16)

    def pack_of(i):
        if i == GRAD:
            load_sources[GRAD_WAY].wait()
            slots_up.wait_recv()
            store_pack(
                packed_out.at[GRAD_WAY],
                pack(source_v.at[GRAD_WAY], slots_v[GRAD_WAY, pl.ds(1, 1), :]),
            )

            @pl.when(section != 0)
            def _():
                rows_dn.start()
        else:
            load_sources[FWD_WAY].wait()
            slots_dn.wait_recv()
            store_pack(
                packed_out.at[FWD_WAY],
                pack(source_v.at[FWD_WAY], slots_v[FWD_WAY, pl.ds(0, 1), :]),
            )

            @pl.when(section != n_pipe - 1)
            def _():
                rows_up.start()

    def relay_all():
        @pl.when(section != 0)
        def _():
            send_grad.start()

        @pl.when(section != n_pipe - 1)
        def _():
            send_fwd.start()

    def tile_of(i):
        if i == GRAD:

            @pl.when(section != n_pipe - 1)
            def _():
                rows_dn.wait_recv()

            @pl.when(section == n_pipe - 1)
            def _():
                load_loss.wait()
                store_pack(packed_in.at[GRAD_WAY], pack(grad_v, slot_v[pl.ds(1, 1), :]))

            grad_tile()
        elif i == FWD:

            @pl.when(section != 0)
            def _():
                rows_up.wait_recv()

            @pl.when(section == 0)
            def _():
                load_fresh.wait()
                store_pack(packed_in.at[FWD_WAY], pack(fwd_v, slot_v[pl.ds(0, 1), :]))

            normed_tile(FWD)
        go(g[i]["tile"])

    def relayed(i):
        if i == GRAD:

            @pl.when(section != n_pipe - 1)
            def _():
                send_grad.wait_recv()
        else:

            @pl.when(section != 0)
            def _():
                send_fwd.wait_recv()

    def own(i):
        arrive(g[i]["tile"])
        rows[i, 0, 0, 0] = tile[i, :, own_cols] + sib_tile[i]
        for name in ("au", "ad") if HOPS_G[i] else ("au", "ad", "ax"):
            go(g[i][name])

    def own_b(i):
        go(g[i]["bu", 0])
        go(g[i]["bd", 0])

    def hop_a(i):
        arrive(g[i]["au"])
        arrive(g[i]["ad"])
        go(g[i]["au2"])
        go(g[i]["ad2"])

    def pair(i):
        if not HOPS_G[i]:
            arrive(g[i]["au"])
            arrive(g[i]["ad"])
        go(g[i]["bu", 1])
        go(g[i]["bd", 1])

    def opposite(i):
        for name in ("au2", "ad2") if HOPS_G[i] else ("ax",):
            arrive(g[i][name])
        go(g[i]["bu", 2])
        go(g[i]["bd", 2])
        go(g[i]["s", 0])

    def forward_up(i, k):
        arrive(g[i]["bu", k])
        go(g[i]["bu2", k])
        if k == 2:
            go(g[i]["s", 2])

    def forward_dn(i, k):
        arrive(g[i]["bd", k])
        go(g[i]["bd2", k])
        if k == 2:
            go(g[i]["s", 1])

    def last_pair(i):
        for k in range(2):
            arrive(g[i]["bu2", k])
            arrive(g[i]["bd2", k])
        go(g[i]["s", 3])

    def last(i):
        arrive(g[i]["bu2", 2])
        arrive(g[i]["bd2", 2])
        go(g[i]["s", 4])

    def handed(i):
        for line in range(5):
            arrive(g[i]["s", line])

    def weights_gu():
        for copy in load_gu:
            copy.wait()

    def weights_d():
        for copy in load_d:
            copy.wait()

    def p1(j, c):
        partial(j, 1, c)
        for k in range(3):
            go(r[j]["sib", k, c])

    def p0(j, c):
        partial(j, 0, c)

    def m0(j):
        arrive(r[j]["sib", 0, 0])
        send_b(j, 0, 3, 0)

    def m1(j):
        arrive(r[j]["sib", 0, 1])
        send_b(j, 1, 3, 1)

    def m2(j):
        arrive(r[j]["sib", 1, 0])
        send_b(j, 2, 2, 0)

    def m3(j):
        arrive(r[j]["sib", 1, 1])
        send_b(j, 3, 1, 1)

    def m4(j):
        arrive(r[j]["b", 0])
        send_b(j, 4, 1, 0, plus=0)

    def m5(j):
        arrive(r[j]["b", 1])
        send_b(j, 5, 2, 1, plus=1)

    def w(j, c):
        arrive(r[j]["sib", 2, c])
        line_sum(j, c)

    def ended(j):
        for c in range(2):
            arrive(r[j]["end", c])

    tasks = dict(
        pack=pack_of,
        tile=tile_of,
        relayed=relayed,
        relay_all=relay_all,
        own=own,
        own_b=own_b,
        fa=hop_a,
        pair=pair,
        opposite=opposite,
        fu=forward_up,
        fd=forward_dn,
        last_pair=last_pair,
        last=last,
        handed=handed,
        gu=gate_up,
        gh=grad_hidden,
        act_rowg=act_rowg,
        act_out=act_out,
        p1=p1,
        p0=p0,
        m0=m0,
        m1=m1,
        m2=m2,
        m3=m3,
        m4=m4,
        m5=m5,
        w=w,
        v=hop_r,
        x=block_sum,
        ended=ended,
        project=project,
        finish_grad=finish_grad,
        finish_fwd=finish_fwd,
        weights_gu=weights_gu,
        weights_d=weights_d,
    )

    inverse = normed_tile(BWD)
    inverse_v[...] = jnp.broadcast_to(inverse, inverse_v.shape)
    pl.semaphore_wait(barrier, 8)

    send_fwd = pltpu.make_async_remote_copy(
        src_ref=handed_fwd.at[0],
        dst_ref=fwd_v,
        send_sem=z_send.at[0],
        recv_sem=z_recv.at[0],
        device_id={"pipe": Z_UP, "tensor": t},
        device_id_type=pl.DeviceIdType.MESH,
    )
    send_grad = pltpu.make_async_remote_copy(
        src_ref=handed_grads.at[0],
        dst_ref=grad_v,
        send_sem=z_send.at[1],
        recv_sem=z_recv.at[1],
        device_id={"pipe": Z_DN, "tensor": t},
        device_id_type=pl.DeviceIdType.MESH,
    )

    slots_dn = pltpu.make_async_remote_copy(
        src_ref=slot.at[0],
        dst_ref=slots_v.at[FWD_WAY],
        send_sem=z_send.at[2],
        recv_sem=z_recv.at[2],
        device_id={"pipe": Z_DN, "tensor": t},
        device_id_type=pl.DeviceIdType.MESH,
    )
    slots_up = pltpu.make_async_remote_copy(
        src_ref=slot.at[0],
        dst_ref=slots_v.at[GRAD_WAY],
        send_sem=z_send.at[3],
        recv_sem=z_recv.at[3],
        device_id={"pipe": Z_UP, "tensor": t},
        device_id_type=pl.DeviceIdType.MESH,
    )
    slots_dn.start()
    slots_up.start()
    rows_up = pltpu.make_async_remote_copy(
        src_ref=packed_out.at[FWD_WAY],
        dst_ref=packed_in.at[FWD_WAY],
        send_sem=z_send.at[4],
        recv_sem=z_recv.at[4],
        device_id={"pipe": Z_UP, "tensor": t},
        device_id_type=pl.DeviceIdType.MESH,
    )
    rows_dn = pltpu.make_async_remote_copy(
        src_ref=packed_out.at[GRAD_WAY],
        dst_ref=packed_in.at[GRAD_WAY],
        send_sem=z_send.at[5],
        recv_sem=z_recv.at[5],
        device_id={"pipe": Z_DN, "tensor": t},
        device_id_type=pl.DeviceIdType.MESH,
    )

    @pl.when(section == 0)
    def _():
        load_fresh.start()

    @pl.when(section == n_pipe - 1)
    def _():
        load_loss.start()

    go(g[BWD]["tile"])
    for copy in load_gu + load_d:
        copy.start()
    for name, *at_ in ORDER:
        tasks[name](*at_)

    for copy in sent:
        copy.wait_send()

    slots_dn.wait_send()
    slots_up.wait_send()

    @pl.when(section != n_pipe - 1)
    def _():
        rows_up.wait_send()
        send_fwd.wait_send()

    @pl.when(section != 0)
    def _():
        rows_dn.wait_send()
        send_grad.wait_send()


def place(fwd_in, grad_in, fwd_out, grad_out, sem):
    copies = [
        pltpu.make_async_copy(fwd_in, fwd_out, sem.at[0]),
        pltpu.make_async_copy(grad_in, grad_out, sem.at[1]),
    ]
    for copy in copies:
        copy.start()
    for copy in copies:
        copy.wait()


def on_device(
    n_pipe,
    fresh_batch,
    handed_forward,
    saved_inputs,
    handed_grads,
    loss_grad,
    norm_gain,
    route_slot,
    route_weight,
    w_gate,
    w_up,
    w_down,
):
    TOKD, D = fresh_batch.shape
    FFD = w_down.shape[1]
    H, C = D // 2, D // 4
    FLAT = SIDE * SIDE * PAIR
    anywhere = pl.BlockSpec(memory_space=pl.ANY)
    vmem = pltpu.VMEM
    dma = pltpu.SemaphoreType.DMA
    shape = jax.ShapeDtypeStruct((1, TOKD, D), BF16)
    inside = vmem((1, TOKD, D), BF16)
    in_vmem = pl.BlockSpec(memory_space=vmem)
    results = pl.pallas_call(
        functools.partial(kernel, n_pipe),
        out_shape=(inside, inside),
        in_specs=[anywhere] * 11,
        out_specs=(in_vmem, in_vmem),
        scratch_shapes=[
            vmem((TOKD, D), BF16),
            vmem((TOKD, D), BF16),
            vmem((TOKD, D), BF16),
            vmem((1, D), F32),
            vmem((2, TOKD), jnp.int32),
            vmem((2, TOKD), F32),
            vmem((2, TOKD, D), BF16),
            vmem((2, 2, TOKD), jnp.int32),
            vmem((2, PAIR, H), BF16),
            vmem((2, PAIR, H), BF16),
            vmem((2, H, 2 * FFD), BF16),
            vmem((2, FFD, H), BF16),
            vmem((2, PAIR, D), F32),
            vmem((3, PAIR, D), BF16),
            vmem((3, PAIR, H), BF16),
            vmem((3, 2, SIDE, SIDE, PAIR, H), BF16),
            vmem((2, FLAT, 2 * FFD), F32),
            vmem((FLAT, FFD), F32),
            vmem((2, FLAT, 2 * FFD), BF16),
            vmem((2, 2, 2, SIDE, SIDE, PAIR, C), BF16),
            vmem((2, 2, SIDE, SIDE, PAIR, C), BF16),
            vmem((2, 6, SIDE, PAIR, C), BF16),
            vmem((2, 6, SIDE, PAIR, C), BF16),
            vmem((2, 2, 2, PAIR, C), F32),
            vmem((2, 2, 3, PAIR, C), BF16),
            vmem((2, 2, 3, PAIR, C), BF16),
            vmem((2, PAIR, D), BF16),
            vmem((PAIR, 128), F32),
            vmem((2, PAIR, D), BF16),
            dma((14,)),
            dma((6,)),
            dma((6,)),
            dma((3, 22)),
            dma((3, 22)),
            dma((2, 20)),
            dma((2, 20)),
        ],
        compiler_params=pltpu.CompilerParams(
            collective_id=0, has_side_effects=True, vmem_limit_bytes=56 * 2**20
        ),
    )(
        fresh_batch,
        handed_forward,
        saved_inputs,
        handed_grads,
        loss_grad,
        norm_gain,
        route_slot,
        route_weight,
        w_gate,
        w_up,
        w_down,
    )
    return pl.pallas_call(
        place,
        out_shape=(shape, shape),
        in_specs=[in_vmem] * 2,
        out_specs=(anywhere, anywhere),
        scratch_shapes=[dma((2,))],
        compiler_params=pltpu.CompilerParams(vmem_limit_bytes=8 * 2**20),
    )(*results)


def solution(mesh):
    placed = (
        P("tensor", None),
        P("pipe", "tensor", None),
        P("pipe", "tensor", None),
        P("pipe", "tensor", None),
        P("tensor", None),
        P("pipe", None),
        P("pipe", None, "tensor"),
        P("pipe", None, "tensor"),
        P("pipe", None, "tensor"),
        P("pipe", None, "tensor"),
        P("pipe", "tensor", None),
    )
    return jax.shard_map(
        functools.partial(on_device, mesh.shape["pipe"]),
        mesh=mesh,
        in_specs=placed,
        out_specs=(P("pipe", "tensor", None), P("pipe", "tensor", None)),
        check_vma=False,
    )
```

```python
import functools

import jax
import jax.numpy as jnp
from jax import lax
from jax.experimental import pallas as pl
from jax.experimental.pallas import tpu as pltpu
from jax.sharding import PartitionSpec as P

LCAP = 8
SIDE = 4
PAIR = 2 * LCAP
EPS = 1e-05
F32 = jnp.float32
BF16 = jnp.bfloat16
BWD, GRAD, FWD = 0, 1, 2
FWD_WAY, GRAD_WAY = 0, 1
ROWG, OUT = 0, 1


def contract_last(left, right):
    return lax.dot_general(left, right, (((1,), (1,)), ((), ())), preferred_element_type=F32)
HOPS_G = (False, True, True)
HOPS_R = (True, False)
ORDER = (
    ("own", 0),
    ("pack", 1),
    ("pack", 2),
    ("own_b", 0),
    ("pair", 0),
    ("opposite", 0),
    ("weights_d",),
    ("tile", 1),
    ("fd", 0, 0),
    ("fu", 0, 0),
    ("own", 1),
    ("fd", 0, 1),
    ("fu", 0, 1),
    ("tile", 2),
    ("own_b", 1),
    ("own", 2),
    ("fa", 1),
    ("weights_gu",),
    ("pair", 1),
    ("last_pair", 0),
    ("fu", 0, 2),
    ("fa", 2),
    ("fd", 0, 2),
    ("opposite", 1),
    ("own_b", 2),
    ("fd", 1, 0),
    ("fu", 1, 0),
    ("fu", 1, 1),
    ("last", 0),
    ("fd", 1, 1),
    ("gu", 0, 0),
    ("fu", 1, 2),
    ("fd", 1, 2),
    ("pair", 2),
    ("opposite", 2),
    ("handed", 0),
    ("gu", 0, 1),
    ("fd", 2, 0),
    ("last_pair", 1),
    ("last", 1),
    ("fu", 2, 0),
    ("gh", 0),
    ("handed", 1),
    ("gh", 1),
    ("relay_all",),
    ("act_rowg",),
    ("p1", 0, 1),
    ("fd", 2, 1),
    ("fu", 2, 1),
    ("p1", 0, 0),
    ("fd", 2, 2),
    ("fu", 2, 2),
    ("p0", 0, 1),
    ("m1", 0),
    ("p0", 0, 0),
    ("m0", 0),
    ("m3", 0),
    ("m2", 0),
    ("last_pair", 2),
    ("last", 2),
    ("gu", 2, 0),
    ("handed", 2),
    ("gu", 2, 1),
    ("act_out",),
    ("m5", 0),
    ("p1", 1, 1),
    ("m4", 0),
    ("p0", 1, 1),
    ("p1", 1, 0),
    ("m1", 1),
    ("p0", 1, 0),
    ("m0", 1),
    ("m3", 1),
    ("m2", 1),
    ("w", 0, 1),
    ("m5", 1),
    ("w", 0, 0),
    ("m4", 1),
    ("v", 0, 0),
    ("v", 0, 1),
    ("w", 1, 1),
    ("w", 1, 0),
    ("x", 0, 0),
    ("x", 0, 1),
    ("ended", 0),
    ("project",),
    ("relayed", 1),
    ("finish_grad",),
    ("relayed", 2),
    ("x", 1, 1),
    ("finish_fwd", 0, 1),
    ("x", 1, 0),
    ("finish_fwd", 1, 1),
    ("finish_fwd", 0, 0),
    ("finish_fwd", 1, 0),
)


def kernel(
    n_pipe,
    fresh,
    handed_fwd,
    saved,
    handed_grads,
    loss_grad,
    gain,
    slot,
    weight,
    w_gate,
    w_up,
    w_down,
    out_fwd,
    out_grad,
    saved_v,
    fwd_v,
    grad_v,
    gain_v,
    slot_v,
    weight_v,
    source_v,
    slots_v,
    packed_out,
    packed_in,
    wgu,
    wd,
    picked,
    tile,
    sib_tile,
    rows,
    acc,
    gh,
    act,
    part,
    sib_part,
    b_out,
    b_in,
    w_sum,
    a_out,
    a_in,
    final,
    inverse_v,
    changes,
    loc_sem,
    z_send,
    z_recv,
    g_send,
    g_recv,
    r_send,
    r_recv,
):
    D = saved.shape[2]
    TOKD = saved.shape[1]
    FFD = w_down.shape[1]
    H = D // 2
    C = D // 4
    LANES = min(1024, H)

    section = lax.axis_index("pipe")
    t = lax.axis_index("tensor")
    core = t % 2
    x = t // (2 * SIDE)
    y = (t // 2) % SIDE
    a = x + core * (y - x)
    b = y + core * (x - y)
    sa = 2 * SIDE - core * (2 * SIDE - 2)
    sb = 2 + core * (2 * SIDE - 2)
    A_UP = ((a + 1) % SIDE) * sa + b * sb + core
    A_OP = ((a + 2) % SIDE) * sa + b * sb + core
    A_DN = ((a + 3) % SIDE) * sa + b * sb + core
    B_UP = a * sa + ((b + 1) % SIDE) * sb + core
    B_DN = a * sa + ((b + 3) % SIDE) * sb + core
    SIB = t + 1 - 2 * core
    Z_UP = (section + 1) % n_pipe
    Z_DN = (section + n_pipe - 1) % n_pipe
    own_cols = pl.ds(pl.multiple_of(core * H, H), H)
    oth = pl.ds(pl.multiple_of((1 - core) * H, H), H)

    def at(tensor):
        return {"pipe": section, "tensor": tensor}

    def local(src, dst, k):
        return pltpu.make_async_copy(src, dst, loc_sem.at[k])

    first = [
        local(saved.at[0], saved_v, 0),
        local(gain, gain_v, 1),
        local(slot.at[0], slot_v, 2),
        local(weight.at[0], weight_v, 3),
    ]
    load_gu = [
        local(w_gate.at[0, own_cols], wgu.at[0, :, pl.ds(0, FFD)], 4),
        local(w_gate.at[0, oth], wgu.at[1, :, pl.ds(0, FFD)], 5),
        local(w_up.at[0, own_cols], wgu.at[0, :, pl.ds(FFD, FFD)], 6),
        local(w_up.at[0, oth], wgu.at[1, :, pl.ds(FFD, FFD)], 7),
    ]
    load_d = [
        local(w_down.at[0, :, own_cols], wd.at[0], 8),
        local(w_down.at[0, :, oth], wd.at[1], 9),
    ]
    load_fresh = local(fresh, fwd_v, 10)
    load_loss = local(loss_grad, grad_v, 11)
    load_sources = [
        local(handed_fwd.at[0], source_v.at[FWD_WAY], 12),
        local(handed_grads.at[0], source_v.at[GRAD_WAY], 13),
    ]
    for copy in first + load_sources:
        copy.start()

    barrier = pltpu.get_barrier_semaphore()
    for tensor in (SIB, A_UP, A_OP, A_DN, B_UP, B_DN):
        pl.semaphore_signal(
            barrier, inc=1, device_id=at(tensor), device_id_type=pl.DeviceIdType.MESH
        )
    for pipe in (Z_UP, Z_DN):
        pl.semaphore_signal(
            barrier,
            inc=1,
            device_id={"pipe": pipe, "tensor": t},
            device_id_type=pl.DeviceIdType.MESH,
        )
    sent = []

    def remote(src, dst, send_sem, recv_sem, tensor):
        copy = pltpu.make_async_remote_copy(
            src_ref=src,
            dst_ref=dst,
            send_sem=send_sem,
            recv_sem=recv_sem,
            device_id=at(tensor),
            device_id_type=pl.DeviceIdType.MESH,
        )
        return copy

    def go(copy):
        copy.start()
        sent.append(copy)
        return copy

    for copy in first:
        copy.wait()

    def row_pick(micro):
        places = lax.broadcasted_iota(jnp.int32, (PAIR, TOKD), 0) - core * LCAP
        slots = jnp.broadcast_to(slot_v[pl.ds(micro, 1), :], (PAIR, TOKD))
        return jnp.where((places == slots) & (places >= 0) & (places < LCAP), 1.0, 0.0)

    def column(row):
        wide = jnp.broadcast_to(row, (TOKD, TOKD))
        eye = lax.broadcasted_iota(jnp.int32, (TOKD, TOKD), 0) == lax.broadcasted_iota(
            jnp.int32, (TOKD, TOKD), 1
        )
        return jnp.sum(jnp.where(eye, wide, 0.0), axis=1, keepdims=True)

    def token_pick(micro):
        slots = column(slot_v[pl.ds(micro, 1), :].astype(F32))
        slots = jnp.broadcast_to(slots, (TOKD, PAIR))
        places = (
            lax.broadcasted_iota(jnp.int32, (TOKD, PAIR), 1) - core * LCAP
        ).astype(F32)
        return jnp.where(
            (places == slots) & (places >= 0.0) & (places < float(LCAP)), 1.0, 0.0
        ).astype(BF16)

    def lanes(k):
        return pl.ds(k * LANES, LANES)

    def pack(source, slots):
        places = lax.broadcasted_iota(jnp.int32, (PAIR, TOKD), 0)
        slots = jnp.broadcast_to(slots, (PAIR, TOKD))
        low = jnp.where((places == slots) & (places < LCAP), 1.0, 0.0).astype(BF16)
        high = jnp.where((places - LCAP == slots) & (slots < LCAP), 1.0, 0.0).astype(BF16)
        parts = []
        for k in range(H // LANES):
            parts.append(
                jnp.dot(low, source[:, lanes(k)], preferred_element_type=F32)
                + jnp.dot(high, source[:, lanes(k + H // LANES)], preferred_element_type=F32)
            )
        return parts

    def store_pack(dst, parts):
        for k, value in enumerate(parts):
            dst[:, lanes(k)] = value.astype(BF16)

    def unpacked(way, k):
        half, k = k // (H // LANES), k % (H // LANES)
        places = lax.broadcasted_iota(jnp.int32, (PAIR, PAIR), 0) - core * LCAP
        origin = lax.broadcasted_iota(jnp.int32, (PAIR, PAIR), 1) - half * LCAP
        pick = jnp.where((places == origin) & (places >= 0) & (places < LCAP), 1.0, 0.0)
        return jnp.dot(
            pick.astype(BF16), packed_in[way, :, lanes(k)], preferred_element_type=F32
        )

    def normed_tile(i):
        pick = row_pick(1).astype(BF16)
        place = 0 if i == BWD else 1
        total = jnp.zeros((PAIR, 1), F32)
        for k in range(D // LANES):
            if i == BWD:
                z = jnp.dot(pick, saved_v[:, lanes(k)], preferred_element_type=F32)
            else:
                z = unpacked(FWD_WAY, k)
            picked[place, :, lanes(k)] = z
            total = total + jnp.sum(z * z, axis=1, keepdims=True)
        inverse = lax.rsqrt(total * (1.0 / D) + EPS)
        for k in range(D // LANES):
            tile[i, :, lanes(k)] = (
                picked[place, :, lanes(k)] * inverse * gain_v[:, lanes(k)]
            ).astype(BF16)
        return inverse

    def grad_tile():
        pick = row_pick(1)
        weights = jnp.sum(
            pick * jnp.broadcast_to(weight_v[pl.ds(1, 1), :], (PAIR, TOKD)),
            axis=1,
            keepdims=True,
        )
        for k in range(D // LANES):
            g = unpacked(GRAD_WAY, k)
            tile[GRAD, :, lanes(k)] = (weights * g).astype(BF16)

    C0, C1 = pl.ds(0, C), pl.ds(C, C)
    PAIR_OF = pl.ds(1, 2)

    def gather(i):
        count = iter(range(22))

        def send(src, dst, tensor):
            m = next(count)
            return remote(src, dst, g_send.at[i, m], g_recv.at[i, m], tensor)

        mine = rows.at[i, 0]
        copies = {
            "tile": send(tile.at[i, :, oth], sib_tile.at[i], SIB),
            "au": send(mine.at[0, 0], mine.at[0, 2], A_UP),
            "ad": send(mine.at[0, 0], mine.at[0, 1], A_DN),
        }
        if HOPS_G[i]:
            copies["au2"] = send(mine.at[0, 2, :, C0], mine.at[0, 3, :, C0], A_UP)
            copies["ad2"] = send(mine.at[0, 1, :, C1], mine.at[0, 3, :, C1], A_DN)
        else:
            copies["ax"] = send(mine.at[0, 0], mine.at[0, 3], A_OP)
        for k, group in enumerate((pl.ds(0, 1), PAIR_OF, pl.ds(3, 1))):
            copies["bu", k] = send(mine.at[0, group], mine.at[2, group], B_UP)
            copies["bd", k] = send(mine.at[0, group], mine.at[1, group], B_DN)
            copies["bu2", k] = send(
                mine.at[2, group, :, C0], mine.at[3, group, :, C0], B_UP
            )
            copies["bd2", k] = send(
                mine.at[1, group, :, C1], mine.at[3, group, :, C1], B_DN
            )
        for line in range(3):
            copies["s", line] = send(mine.at[line], rows.at[i, 1, :, line], SIB)
        first = pl.ds(0, 3)
        copies["s", 3] = send(mine.at[3, first], rows.at[i, 1, first, 3], SIB)
        copies["s", 4] = send(mine.at[3, 3], rows.at[i, 1, 3, 3], SIB)
        return copies

    g = [gather(i) for i in range(3)]

    def reduction(j):
        count = iter(range(20))

        def send(src, dst, tensor):
            m = next(count)
            return remote(src, dst, r_send.at[j, m], r_recv.at[j, m], tensor)

        copies = {}
        for k, lines in enumerate((pl.ds(3, 1), PAIR_OF, pl.ds(0, 1))):
            for c in range(2):
                copies["sib", k, c] = send(
                    part.at[j, 1, c, lines], sib_part.at[j, c, lines], SIB
                )
        for m, tensor in enumerate((B_UP, B_DN, B_DN, B_UP, B_UP, B_DN)):
            copies["b", m] = send(b_out.at[j, m], b_in.at[j, m], tensor)
        for c in range(2):
            far = (A_UP, A_DN)[c] if HOPS_R[j] else A_OP
            for m, tensor in enumerate((A_UP, A_DN, far)):
                copies["a", c, m] = send(a_out.at[j, c, m], a_in.at[j, c, m], tensor)
            cols = pl.ds(pl.multiple_of(core * H + c * C, C), C)
            copies["end", c] = send(final.at[j, :, cols], final.at[j, :, cols], SIB)
        return copies

    r = [reduction(j) for j in range(2)]

    def arrive(copy):
        copy.wait_recv()

    KC = C
    FLAT = SIDE * SIDE * PAIR

    def accumulate(dst, i, h, product):
        for c in range(2):
            cols = pl.ds(c * KC, KC)
            term = product(rows[i, h, :, :, :, cols].reshape(FLAT, KC), h, cols)
            dst[...] = term if (h, c) == (0, 0) else dst[...] + term

    def by_gate_up(left, h, cols):
        return jnp.dot(left, wgu[h, cols, :], preferred_element_type=F32)

    def by_down(left, h, cols):
        return contract_last(left, wd[h, :, cols])

    def gate_up(i, h):
        accumulate(acc.at[0 if i == BWD else 1], i, h, by_gate_up)

    def grad_hidden(h):
        accumulate(gh, GRAD, h, by_down)

    GATE, UP = pl.ds(0, FFD), pl.ds(FFD, FFD)

    def act_rowg():
        gate = acc[0, :, GATE]
        sigma = jax.nn.sigmoid(gate)
        grad = gh[...]
        act[0, :, GATE] = (
            grad * acc[0, :, UP] * sigma * (1.0 + gate * (1.0 - sigma))
        ).astype(BF16)
        act[0, :, UP] = (grad * (gate * sigma)).astype(BF16)

    def act_out():
        gate = acc[1, :, GATE]
        act[1, :, GATE] = (gate * jax.nn.sigmoid(gate) * acc[1, :, UP]).astype(BF16)

    NC = C // 3 if C % 384 == 0 else C

    def partial(j, h, c):
        for n in range(C // NC):
            if j == OUT:
                term = jnp.dot(
                    act[1, :, GATE],
                    wd[h, :, pl.ds(c * C + n * NC, NC)],
                    preferred_element_type=F32,
                )
            else:
                term = contract_last(act[0], wgu[h, pl.ds(c * C + n * NC, NC), :])
            term = term.astype(BF16).reshape(SIDE, SIDE, PAIR, NC)
            cols = pl.ds(n * NC, NC)
            if h == 0:
                part[j, 0, c, :, :, :, cols] = term
            else:
                for line in range(SIDE):
                    part[j, 1, c, line, :, :, cols] = term[:, line]

    def chip_sum(j, line, c):
        return part[j, 0, c, line].astype(F32) + sib_part[j, c, line].astype(F32)

    def send_b(j, m, line, c, plus=None):
        value = chip_sum(j, line, c)
        if plus is not None:
            value = value + b_in[j, plus].astype(F32)
        b_out[j, m] = value.astype(BF16)
        go(r[j]["b", m])

    def line_sum(j, c):
        one, two = 2 + c, 4 + c
        arrive(r[j]["b", one])
        arrive(r[j]["b", two])
        total = chip_sum(j, 0, c) + b_in[j, one].astype(F32) + b_in[j, two].astype(F32)
        w_sum[j, c, 0] = total[0]
        if HOPS_R[j]:
            w_sum[j, c, 1] = total[1 + c]
            a_out[j, c, 2] = total[3].astype(BF16)
            a_out[j, c, 1 - c] = total[2 - c].astype(BF16)
            go(r[j]["a", c, 2])
            go(r[j]["a", c, 1 - c])
        else:
            a_out[j, c] = total[1:].astype(BF16)
            for m in range(3):
                go(r[j]["a", c, m])

    def hop_r(j, c):
        arrive(r[j]["a", c, 2])
        a_out[j, c, c] = (w_sum[j, c, 1] + a_in[j, c, 2].astype(F32)).astype(BF16)
        go(r[j]["a", c, c])

    def block_sum(j, c):
        total = w_sum[j, c, 0]
        for m in range(2) if HOPS_R[j] else range(3):
            arrive(r[j]["a", c, m])
            total = total + a_in[j, c, m].astype(F32)
        final[j, :, pl.ds(pl.multiple_of(core * H + c * C, C), C)] = total.astype(BF16)
        go(r[j]["end", c])

    def part_lanes(h, c, k):
        start = (core if h == 0 else 1 - core) * H
        return pl.ds(pl.multiple_of(start + c * C + k * NC, NC), NC)

    def project():
        inverse = inverse_v[:, pl.ds(0, 1)]
        total = jnp.zeros((PAIR, 1), F32)
        for k in range(D // LANES):
            adjusted = final[ROWG, :, lanes(k)].astype(F32) * gain_v[:, lanes(k)]
            total = total + jnp.sum(adjusted * picked[0, :, lanes(k)], axis=1, keepdims=True)
        factor = (inverse * inverse * inverse) * (total * (1.0 / D))
        for k in range(D // LANES):
            adjusted = final[ROWG, :, lanes(k)].astype(F32) * gain_v[:, lanes(k)]
            change = adjusted * inverse - picked[0, :, lanes(k)] * factor
            high = change.astype(BF16)
            changes[0, :, lanes(k)] = high
            changes[1, :, lanes(k)] = (change - high.astype(F32)).astype(BF16)

    def finish_grad():
        pick = token_pick(1)
        for k in range(D // LANES):
            cols = lanes(k)
            out_grad[0, :, cols] = (
                grad_v[:, cols].astype(F32)
                + jnp.dot(pick, changes[0, :, cols], preferred_element_type=F32)
                + jnp.dot(pick, changes[1, :, cols], preferred_element_type=F32)
            ).astype(BF16)

    def finish_fwd(h, c):
        if h == 1:
            arrive(r[OUT]["end", c])
        pick = token_pick(0)
        scale = column(weight_v[pl.ds(0, 1), :])

        for k in range(C // NC):
            cols = part_lanes(h, c, k)
            spread = jnp.dot(pick, final[OUT, :, cols], preferred_element_type=F32)
            out_fwd[0, :, cols] = (fwd_v[:, cols].astype(F32) + scale * spread).astype(BF16)

    def pack_of(i):
        if i == GRAD:
            load_sources[GRAD_WAY].wait()
            slots_up.wait_recv()
            store_pack(
                packed_out.at[GRAD_WAY],
                pack(source_v.at[GRAD_WAY], slots_v[GRAD_WAY, pl.ds(1, 1), :]),
            )

            @pl.when(section != 0)
            def _():
                rows_dn.start()
        else:
            load_sources[FWD_WAY].wait()
            slots_dn.wait_recv()
            store_pack(
                packed_out.at[FWD_WAY],
                pack(source_v.at[FWD_WAY], slots_v[FWD_WAY, pl.ds(0, 1), :]),
            )

            @pl.when(section != n_pipe - 1)
            def _():
                rows_up.start()

    def relay_all():
        @pl.when(section != 0)
        def _():
            send_grad.start()

        @pl.when(section != n_pipe - 1)
        def _():
            send_fwd.start()

    def tile_of(i):
        if i == GRAD:

            @pl.when(section != n_pipe - 1)
            def _():
                rows_dn.wait_recv()

            @pl.when(section == n_pipe - 1)
            def _():
                load_loss.wait()
                store_pack(packed_in.at[GRAD_WAY], pack(grad_v, slot_v[pl.ds(1, 1), :]))

            grad_tile()
        elif i == FWD:

            @pl.when(section != 0)
            def _():
                rows_up.wait_recv()

            @pl.when(section == 0)
            def _():
                load_fresh.wait()
                store_pack(packed_in.at[FWD_WAY], pack(fwd_v, slot_v[pl.ds(0, 1), :]))

            normed_tile(FWD)
        go(g[i]["tile"])

    def relayed(i):
        if i == GRAD:

            @pl.when(section != n_pipe - 1)
            def _():
                send_grad.wait_recv()
        else:

            @pl.when(section != 0)
            def _():
                send_fwd.wait_recv()

    def own(i):
        arrive(g[i]["tile"])
        rows[i, 0, 0, 0] = tile[i, :, own_cols] + sib_tile[i]
        for name in ("au", "ad") if HOPS_G[i] else ("au", "ad", "ax"):
            go(g[i][name])

    def own_b(i):
        go(g[i]["bu", 0])
        go(g[i]["bd", 0])

    def hop_a(i):
        arrive(g[i]["au"])
        arrive(g[i]["ad"])
        go(g[i]["au2"])
        go(g[i]["ad2"])

    def pair(i):
        if not HOPS_G[i]:
            arrive(g[i]["au"])
            arrive(g[i]["ad"])
        go(g[i]["bu", 1])
        go(g[i]["bd", 1])

    def opposite(i):
        for name in ("au2", "ad2") if HOPS_G[i] else ("ax",):
            arrive(g[i][name])
        go(g[i]["bu", 2])
        go(g[i]["bd", 2])
        go(g[i]["s", 0])

    def forward_up(i, k):
        arrive(g[i]["bu", k])
        go(g[i]["bu2", k])
        if k == 2:
            go(g[i]["s", 2])

    def forward_dn(i, k):
        arrive(g[i]["bd", k])
        go(g[i]["bd2", k])
        if k == 2:
            go(g[i]["s", 1])

    def last_pair(i):
        for k in range(2):
            arrive(g[i]["bu2", k])
            arrive(g[i]["bd2", k])
        go(g[i]["s", 3])

    def last(i):
        arrive(g[i]["bu2", 2])
        arrive(g[i]["bd2", 2])
        go(g[i]["s", 4])

    def handed(i):
        for line in range(5):
            arrive(g[i]["s", line])

    def weights_gu():
        for copy in load_gu:
            copy.wait()

    def weights_d():
        for copy in load_d:
            copy.wait()

    def p1(j, c):
        partial(j, 1, c)
        for k in range(3):
            go(r[j]["sib", k, c])

    def p0(j, c):
        partial(j, 0, c)

    def m0(j):
        arrive(r[j]["sib", 0, 0])
        send_b(j, 0, 3, 0)

    def m1(j):
        arrive(r[j]["sib", 0, 1])
        send_b(j, 1, 3, 1)

    def m2(j):
        arrive(r[j]["sib", 1, 0])
        send_b(j, 2, 2, 0)

    def m3(j):
        arrive(r[j]["sib", 1, 1])
        send_b(j, 3, 1, 1)

    def m4(j):
        arrive(r[j]["b", 0])
        send_b(j, 4, 1, 0, plus=0)

    def m5(j):
        arrive(r[j]["b", 1])
        send_b(j, 5, 2, 1, plus=1)

    def w(j, c):
        arrive(r[j]["sib", 2, c])
        line_sum(j, c)

    def ended(j):
        for c in range(2):
            arrive(r[j]["end", c])

    tasks = dict(
        pack=pack_of,
        tile=tile_of,
        relayed=relayed,
        relay_all=relay_all,
        own=own,
        own_b=own_b,
        fa=hop_a,
        pair=pair,
        opposite=opposite,
        fu=forward_up,
        fd=forward_dn,
        last_pair=last_pair,
        last=last,
        handed=handed,
        gu=gate_up,
        gh=grad_hidden,
        act_rowg=act_rowg,
        act_out=act_out,
        p1=p1,
        p0=p0,
        m0=m0,
        m1=m1,
        m2=m2,
        m3=m3,
        m4=m4,
        m5=m5,
        w=w,
        v=hop_r,
        x=block_sum,
        ended=ended,
        project=project,
        finish_grad=finish_grad,
        finish_fwd=finish_fwd,
        weights_gu=weights_gu,
        weights_d=weights_d,
    )

    inverse = normed_tile(BWD)
    inverse_v[...] = jnp.broadcast_to(inverse, inverse_v.shape)
    pl.semaphore_wait(barrier, 8)

    send_fwd = pltpu.make_async_remote_copy(
        src_ref=handed_fwd.at[0],
        dst_ref=fwd_v,
        send_sem=z_send.at[0],
        recv_sem=z_recv.at[0],
        device_id={"pipe": Z_UP, "tensor": t},
        device_id_type=pl.DeviceIdType.MESH,
    )
    send_grad = pltpu.make_async_remote_copy(
        src_ref=handed_grads.at[0],
        dst_ref=grad_v,
        send_sem=z_send.at[1],
        recv_sem=z_recv.at[1],
        device_id={"pipe": Z_DN, "tensor": t},
        device_id_type=pl.DeviceIdType.MESH,
    )

    slots_dn = pltpu.make_async_remote_copy(
        src_ref=slot.at[0],
        dst_ref=slots_v.at[FWD_WAY],
        send_sem=z_send.at[2],
        recv_sem=z_recv.at[2],
        device_id={"pipe": Z_DN, "tensor": t},
        device_id_type=pl.DeviceIdType.MESH,
    )
    slots_up = pltpu.make_async_remote_copy(
        src_ref=slot.at[0],
        dst_ref=slots_v.at[GRAD_WAY],
        send_sem=z_send.at[3],
        recv_sem=z_recv.at[3],
        device_id={"pipe": Z_UP, "tensor": t},
        device_id_type=pl.DeviceIdType.MESH,
    )
    slots_dn.start()
    slots_up.start()
    rows_up = pltpu.make_async_remote_copy(
        src_ref=packed_out.at[FWD_WAY],
        dst_ref=packed_in.at[FWD_WAY],
        send_sem=z_send.at[4],
        recv_sem=z_recv.at[4],
        device_id={"pipe": Z_UP, "tensor": t},
        device_id_type=pl.DeviceIdType.MESH,
    )
    rows_dn = pltpu.make_async_remote_copy(
        src_ref=packed_out.at[GRAD_WAY],
        dst_ref=packed_in.at[GRAD_WAY],
        send_sem=z_send.at[5],
        recv_sem=z_recv.at[5],
        device_id={"pipe": Z_DN, "tensor": t},
        device_id_type=pl.DeviceIdType.MESH,
    )

    @pl.when(section == 0)
    def _():
        load_fresh.start()

    @pl.when(section == n_pipe - 1)
    def _():
        load_loss.start()

    go(g[BWD]["tile"])
    for copy in load_gu + load_d:
        copy.start()
    for name, *at_ in ORDER:
        tasks[name](*at_)

    for copy in sent:
        copy.wait_send()

    slots_dn.wait_send()
    slots_up.wait_send()

    @pl.when(section != n_pipe - 1)
    def _():
        rows_up.wait_send()
        send_fwd.wait_send()

    @pl.when(section != 0)
    def _():
        rows_dn.wait_send()
        send_grad.wait_send()


def place(fwd_in, grad_in, fwd_out, grad_out, sem):
    copies = [
        pltpu.make_async_copy(fwd_in, fwd_out, sem.at[0]),
        pltpu.make_async_copy(grad_in, grad_out, sem.at[1]),
    ]
    for copy in copies:
        copy.start()
    for copy in copies:
        copy.wait()


def on_device(
    n_pipe,
    fresh_batch,
    handed_forward,
    saved_inputs,
    handed_grads,
    loss_grad,
    norm_gain,
    route_slot,
    route_weight,
    w_gate,
    w_up,
    w_down,
):
    TOKD, D = fresh_batch.shape
    FFD = w_down.shape[1]
    H, C = D // 2, D // 4
    FLAT = SIDE * SIDE * PAIR
    anywhere = pl.BlockSpec(memory_space=pl.ANY)
    vmem = pltpu.VMEM
    dma = pltpu.SemaphoreType.DMA
    shape = jax.ShapeDtypeStruct((1, TOKD, D), BF16)
    inside = vmem((1, TOKD, D), BF16)
    in_vmem = pl.BlockSpec(memory_space=vmem)
    results = pl.pallas_call(
        functools.partial(kernel, n_pipe),
        out_shape=(inside, inside),
        in_specs=[anywhere] * 11,
        out_specs=(in_vmem, in_vmem),
        scratch_shapes=[
            vmem((TOKD, D), BF16),
            vmem((TOKD, D), BF16),
            vmem((TOKD, D), BF16),
            vmem((1, D), F32),
            vmem((2, TOKD), jnp.int32),
            vmem((2, TOKD), F32),
            vmem((2, TOKD, D), BF16),
            vmem((2, 2, TOKD), jnp.int32),
            vmem((2, PAIR, H), BF16),
            vmem((2, PAIR, H), BF16),
            vmem((2, H, 2 * FFD), BF16),
            vmem((2, FFD, H), BF16),
            vmem((2, PAIR, D), F32),
            vmem((3, PAIR, D), BF16),
            vmem((3, PAIR, H), BF16),
            vmem((3, 2, SIDE, SIDE, PAIR, H), BF16),
            vmem((2, FLAT, 2 * FFD), F32),
            vmem((FLAT, FFD), F32),
            vmem((2, FLAT, 2 * FFD), BF16),
            vmem((2, 2, 2, SIDE, SIDE, PAIR, C), BF16),
            vmem((2, 2, SIDE, SIDE, PAIR, C), BF16),
            vmem((2, 6, SIDE, PAIR, C), BF16),
            vmem((2, 6, SIDE, PAIR, C), BF16),
            vmem((2, 2, 2, PAIR, C), F32),
            vmem((2, 2, 3, PAIR, C), BF16),
            vmem((2, 2, 3, PAIR, C), BF16),
            vmem((2, PAIR, D), BF16),
            vmem((PAIR, 128), F32),
            vmem((2, PAIR, D), BF16),
            dma((14,)),
            dma((6,)),
            dma((6,)),
            dma((3, 22)),
            dma((3, 22)),
            dma((2, 20)),
            dma((2, 20)),
        ],
        compiler_params=pltpu.CompilerParams(
            collective_id=0, has_side_effects=True, vmem_limit_bytes=56 * 2**20
        ),
    )(
        fresh_batch,
        handed_forward,
        saved_inputs,
        handed_grads,
        loss_grad,
        norm_gain,
        route_slot,
        route_weight,
        w_gate,
        w_up,
        w_down,
    )
    return pl.pallas_call(
        place,
        out_shape=(shape, shape),
        in_specs=[in_vmem] * 2,
        out_specs=(anywhere, anywhere),
        scratch_shapes=[dma((2,))],
        compiler_params=pltpu.CompilerParams(vmem_limit_bytes=8 * 2**20),
    )(*results)


def solution(mesh):
    placed = (
        P("tensor", None),
        P("pipe", "tensor", None),
        P("pipe", "tensor", None),
        P("pipe", "tensor", None),
        P("tensor", None),
        P("pipe", None),
        P("pipe", None, "tensor"),
        P("pipe", None, "tensor"),
        P("pipe", None, "tensor"),
        P("pipe", None, "tensor"),
        P("pipe", "tensor", None),
    )
    return jax.shard_map(
        functools.partial(on_device, mesh.shape["pipe"]),
        mesh=mesh,
        in_specs=placed,
        out_specs=(P("pipe", "tensor", None), P("pipe", "tensor", None)),
        check_vma=False,
    )
```
